256 devices in a mesh: snode: 16 (over z, core), rhs: 16 (over x, y).
Axes of the slice: x: 4, y: 4, z: 8, core: 2. Of those that a mesh axis runs over, the one named last changes fastest.
Arguments:
- leaf_inv: bfloat16 [64, 512, 512], P('snode', 'rhs'), as said below
- leaf_panel: bfloat16 [64, 1024, 512], P('snode', 'rhs'), may hold values from -0.0625 to 0.0625
- leaf_rows: int32 [64, 1024], P('snode'), may hold values from 0 to 4095, as said below
- leaf_loads: bfloat16 [64, 512, 4096], P('snode', None, 'rhs'), may hold values from -6 to 6
- top_inv: bfloat16 [4096, 4096], P('snode', 'rhs'), as said below
- top_loads: bfloat16 [4096, 4096], P('snode', 'rhs'), may hold values from -6 to 6
Outputs:
- leaf_solution: float32 [64, 512, 4096], P('snode', None, 'rhs')
- top_solution: float32 [4096, 4096], P('snode', 'rhs')
The draws below stay inside these ranges and needn't reach their ends.
Inputs may be any that keep to these rules, and one draw needn't show every extreme that they name: `leaf_rows`: the indices of one leaf are distinct; each aligned group of 4 consecutive leaves names every separator row exactly once. `leaf_inv`: lower triangular, diagonal between 0.6 and 1.4. `top_inv`: lower triangular, diagonal between 0.6 and 1.4.
All inputs are finite; a program needn't handle non-finite values.
Results may differ from the reference program's by a relative error of at most 0.0045.
Values may be sent and summed in bfloat16 or wider, within the bound.
No kernel may reach another device: no remote copies, remote signals or barrier semaphores. Data moves between devices by JAX's collectives and lax.ppermute only.
A program may use at most 64 MiB of HBM per device.

```python
import math
import jax
import jax.numpy as jnp
from jax import lax

W = 512
R = 1024
W2 = 4096
LEAVES = 64
NRHS = 4096


def triangle(key, count, order, rough):
    diag_key = jax.random.fold_in(key, 11)
    upper = lax.broadcasted_iota(jnp.int32, (order, order), 0)
    lower = lax.broadcasted_iota(jnp.int32, (order, order), 1)
    diagonal = jax.random.uniform(diag_key, (count, order, 1), jnp.float32, 0.6, 1.4)
    offside = rough * (0.5 / math.sqrt(order))
    result = jnp.where(upper > lower, offside, jnp.where(upper == lower, diagonal, 0.0))
    return result.astype(jnp.bfloat16)


def draw_leaf_inv(key, part):
    key = jax.random.fold_in(key, 1)
    rough = jax.random.normal(key, (LEAVES, W, W), jnp.float32)
    return triangle(key, LEAVES, W, rough)


def draw_top_inv(key, part):
    key = jax.random.fold_in(key, 2)
    rough = jax.random.normal(key, (1, W2, W2), jnp.float32)
    return triangle(key, 1, W2, rough)[0]


def draw_leaf_rows(key, part):
    key = jax.random.fold_in(key, 3)
    groups = LEAVES // (W2 // R)
    keys = jax.random.split(key, groups)
    orders = jax.vmap(lambda one_key: jax.random.permutation(one_key, W2))(keys)
    return orders.reshape(LEAVES, R).astype(jnp.int32)


def shard_levels(key, dims, shards, low, top_value):
    level = 1.0
    for axis_at, parts in shards:
        steps = jax.random.uniform(jax.random.fold_in(jax.random.fold_in(key, 6), axis_at), (parts,), jnp.float32, low / len(shards), top_value / len(shards))
        level = level * jnp.repeat(jnp.exp(steps), dims[axis_at] // parts).reshape((-1,) + (1,) * (len(dims) - 1 - axis_at))
    return level


def normal_values(key, extent, scale, most, pieces=(), dtype=jnp.bfloat16):
    level = shard_levels(key, extent, pieces, -0.22, 0.18) if pieces else 1.0
    values = jax.random.normal(key, extent, jnp.float32) * scale * level
    return jnp.minimum(jnp.maximum(values, -most), most).astype(dtype)


def setup_inputs(seed: int = 0) -> dict:
    seeds = jax.random.split(jax.random.key(seed), 7)
    return {
        "leaf_inv": draw_leaf_inv(jax.random.fold_in(seeds[6], 71), 0),
        "leaf_panel": normal_values(seeds[1], (LEAVES, R, W), (W * LEAVES * R // W2) ** -0.5, 0.0625, ((0, 16), (1, 16))),
        "leaf_rows": draw_leaf_rows(jax.random.fold_in(seeds[6], 71), 0),
        "leaf_loads": normal_values(seeds[3], (LEAVES, W, NRHS), 1.0, 6.0, ((0, 16), (2, 16))),
        "top_inv": draw_top_inv(jax.random.fold_in(seeds[6], 71), 0),
        "top_loads": normal_values(seeds[5], (W2, NRHS), 1.0, 6.0, ((0, 16), (1, 16))),
    }


def reference(leaf_inv, leaf_panel, leaf_rows, leaf_loads, top_inv, top_loads):
    def forward_step(update, items):
        inverse, panel, rows, loads = items
        forward = jnp.dot(inverse, loads, preferred_element_type=jnp.float32).astype(jnp.bfloat16)
        partial_value = jnp.dot(panel, forward, preferred_element_type=jnp.float32)
        return update.at[rows].add(partial_value), forward

    start = jnp.zeros((W2, NRHS), jnp.float32)
    update, forward_leaf = lax.scan(forward_step, start, (leaf_inv, leaf_panel, leaf_rows, leaf_loads))
    reduced = (top_loads.astype(jnp.float32) - update).astype(jnp.bfloat16)
    forward_top = jnp.dot(top_inv, reduced, preferred_element_type=jnp.float32).astype(jnp.bfloat16)
    top_solution = jnp.dot(top_inv.T, forward_top, preferred_element_type=jnp.float32)
    top_rounded = top_solution.astype(jnp.bfloat16)

    def backward_step(items):
        inverse, panel, rows, forward = items
        picked = top_rounded[rows]
        back = forward.astype(jnp.float32) - jnp.dot(panel.T, picked, preferred_element_type=jnp.float32)
        back = back.astype(jnp.bfloat16)
        return jnp.dot(inverse.T, back, preferred_element_type=jnp.float32)

    leaf_solution = lax.map(backward_step, (leaf_inv, leaf_panel, leaf_rows, forward_leaf))
    return leaf_solution, top_solution
```

```python
import jax
import jax.numpy as jnp
from jax import lax
from jax.experimental import pallas as pl
from jax.experimental.pallas import tpu as pltpu
from jax.sharding import PartitionSpec as P

BF = jnp.bfloat16
F32 = jnp.float32
OFFSETS = (0, 3, 1, 2)
Z_OFFSETS = (0, 7, 1, 6, 2, 5, 3, 4)
ZS, XS, YS, CORES = 8, 4, 4, 2
VMEM = pl.BlockSpec(memory_space=pltpu.VMEM)
SMEM = pl.BlockSpec(memory_space=pltpu.SMEM)
PARAMS = pltpu.CompilerParams(vmem_limit_bytes=50 * 1024 * 1024)


def move_rhs(a, dx, dy):
    pairs = [(4 * x + y, 4 * ((x + dx) % 4) + (y + dy) % 4) for x in range(XS) for y in range(YS)]
    return lax.ppermute(a, "rhs", pairs)


def move_z(a, d):
    return lax.ppermute(a, "snode", [(i, (i + 2 * d) % 16) for i in range(16)])


def swap_core(a):
    return lax.ppermute(a, "snode", [(i, i ^ 1) for i in range(16)])


def ring_of_four(a, move):
    half = a.shape[0] // 2
    before, after = move(a, 1), move(a, -1)
    return [a, before, after, move(before[:half], 1), move(after[half:], -1)]


def torus_gather(first, second):
    along_x = lambda a, d: move_rhs(a, d, 0)
    along_y = lambda a, d: move_rhs(a, 0, d)
    near = jnp.concatenate(ring_of_four(first, along_y), axis=0)
    near2 = jnp.concatenate(ring_of_four(second, along_x), axis=0)
    return ring_of_four(near, along_x) + ring_of_four(near2, along_y)


def gather_z(a):
    rows = a.shape[0]
    chunks = []
    for part in (a[: rows // 2], a[rows // 2 :]):
        up = down = part
        got = [part]
        for _ in range(3):
            up, down = move_z(up, 1), move_z(down, -1)
            got += [up, down]
        half = part.shape[0] // 2
        got.append(jnp.concatenate([move_z(up[:half], 1), move_z(down[half:], -1)], axis=0))
        chunks.append(jnp.stack(got))
    return jnp.concatenate(chunks, axis=1)


def each_block(pieces, x, y, per):
    for half in range(2):
        group = pieces[5 * half : 5 * half + 5]
        for far in range(4):
            for near in range(4):
                if far < 3:
                    piece, at = group[far], near * per
                else:
                    piece, at = (group[3], near * per) if near < 2 else (group[4], (near - 2) * per)
                a, b = (OFFSETS[far], OFFSETS[near]) if half == 0 else (OFFSETS[near], OFFSETS[far])
                yield half, piece, at, lax.rem(x + a, 4), lax.rem(y + b, 4)


def forward_kernel(place, rows, loads, *refs):
    pieces, (inv, panel, forward, mine, other, partial_value, update) = refs[:10], refs[10:]
    x, y = place[2], place[3]
    for half, piece, at, bx, by in each_block(pieces, x, y, 2):
        r = 4 * bx + by
        for leaf in range(2):
            inv[2 * half + leaf, pl.ds(pl.multiple_of(r * 32, 32), 32), :] = piece[at + leaf, :32, :]
            panel[2 * half + leaf, pl.ds(pl.multiple_of(r * 64, 64), 64), :] = piece[at + leaf, 32:, :]
    for leaf in range(4):
        value = jnp.dot(inv[leaf], loads[leaf], preferred_element_type=F32).astype(BF)
        forward[leaf] = value
        partial_value[...] = jnp.dot(panel[leaf], value, preferred_element_type=F32)

        @pl.loop(0, 1024 // 16)
        def _(step):
            first = pl.multiple_of(step * 16, 16)
            for k in range(16):
                row = rows[leaf * 1024 + first + k]
                update[pl.ds(row, 1), :] = partial_value[pl.ds(first + k, 1), :]

    mine[...] = update[:2048, :]
    other[...] = update[2048:, :]


def top_kernel(place, reduced_mine, reduced_other, *refs):
    pieces, (mine, other, block, reduced) = refs[:10], refs[10:]
    z, c, x, y = place[0], place[1], place[2], place[3]
    for half, piece, at, bx, by in each_block(pieces, x, y, 128):
        r = 4 * bx + by
        block[half * 128 : half * 128 + 128, pl.ds(pl.multiple_of(r * 256, 256), 256)] = piece[at : at + 128, :]
    for k, offset in enumerate(Z_OFFSETS):
        chip = lax.rem(z + offset, 8)
        reduced[pl.ds(pl.multiple_of((2 * chip + c) * 256, 256), 256), :] = reduced_mine[k]
        reduced[pl.ds(pl.multiple_of((2 * chip + 1 - c) * 256, 256), 256), :] = reduced_other[k]
    forward = jnp.dot(block[...], reduced[...], preferred_element_type=F32).astype(BF)
    for chip in range(8):
        for out, core in ((mine, c), (other, 1 - c)):
            columns = block[:, pl.ds(pl.multiple_of((2 * chip + core) * 256, 256), 256)]
            out[chip] = lax.dot_general(columns, forward, (((0,), (0,)), ((), ())), preferred_element_type=F32)


def backward_kernel(rows, inv, panel, forward, top_mine, top_other, out, top, picked):
    for k in range(8):
        top[k * 256 : k * 256 + 256, :] = top_mine[k].astype(F32)
        top[2048 + k * 256 : 2048 + k * 256 + 256, :] = top_other[k].astype(F32)
    for leaf in range(4):

        @pl.loop(0, 1024 // 16)
        def _(step):
            first = pl.multiple_of(step * 16, 16)
            for k in range(16):
                row = rows[leaf * 1024 + first + k]
                picked[pl.ds(first + k, 1), :] = top[pl.ds(row, 1), :]

        through = lax.dot_general(
            panel[leaf], picked[...].astype(BF), (((0,), (0,)), ((), ())), preferred_element_type=F32
        )
        value = (forward[leaf].astype(F32) - through).astype(BF)
        out[leaf] = lax.dot_general(inv[leaf], value, (((0,), (0,)), ((), ())), preferred_element_type=F32)


def reduce_z(mine, other):
    groups = [[2 * z + c for z in range(ZS)] for c in range(CORES)]
    chip = (mine + swap_core(other)).astype(BF)
    got = lax.all_to_all(chip, "snode", 0, 0, axis_index_groups=groups)
    return jnp.sum(got.astype(F32), axis=0)


def per_device(leaf_inv, leaf_panel, leaf_rows, leaf_loads, top_inv, top_loads):
    s, r = lax.axis_index("snode"), lax.axis_index("rhs")
    z, c, x, y = s // 2, s % 2, r // 4, r % 4
    place = jnp.stack([z, c, x, y]).astype(jnp.int32)
    own_core = ((leaf_rows // 256) % 2) == c
    side = jnp.where(own_core, 0, 2048) + leaf_rows % 256
    chip = leaf_rows // 512
    send_rows = (side + chip * 256).reshape(-1)
    away = (chip - z) % 8
    slot = sum(jnp.where(away == k, Z_OFFSETS.index(k), 0) for k in range(8))
    pick_rows = (side + slot * 256).reshape(-1)

    factors = jnp.concatenate([leaf_inv, leaf_panel], axis=1)
    pieces = torus_gather(factors[:2], factors[2:])
    inv, panel, forward, mine, other = pl.pallas_call(
        forward_kernel,
        out_shape=(
            jax.ShapeDtypeStruct((4, 512, 512), BF),
            jax.ShapeDtypeStruct((4, 1024, 512), BF),
            jax.ShapeDtypeStruct((4, 512, 256), BF),
            jax.ShapeDtypeStruct((2048, 256), F32),
            jax.ShapeDtypeStruct((2048, 256), F32),
        ),
        in_specs=[SMEM, SMEM] + [VMEM] * 11,
        out_specs=[VMEM] * 5,
        scratch_shapes=[pltpu.VMEM((1024, 256), F32), pltpu.VMEM((4096, 256), F32)],
        compiler_params=PARAMS,
        cost_estimate=pl.CostEstimate(flops=2 * 10**9, bytes_accessed=20 * 2**20, transcendentals=0),
        name="leaf_forward",
    )(place, send_rows, leaf_loads, *pieces)

    top_pieces = torus_gather(top_inv[:128], top_inv[128:])
    update = reduce_z(mine.reshape(8, 256, 256), other.reshape(8, 256, 256))
    reduced = (top_loads.astype(F32) - update).astype(BF)
    reduced_mine = gather_z(reduced)
    reduced_other = swap_core(reduced_mine)
    top_term, top_term_other = pl.pallas_call(
        top_kernel,
        out_shape=(jax.ShapeDtypeStruct((8, 256, 256), F32),) * 2,
        in_specs=[SMEM] + [VMEM] * 12,
        out_specs=[VMEM] * 2,
        scratch_shapes=[pltpu.VMEM((256, 4096), BF), pltpu.VMEM((4096, 256), BF)],
        compiler_params=PARAMS,
        cost_estimate=pl.CostEstimate(flops=10**9, bytes_accessed=8 * 2**20, transcendentals=0),
        name="top_solve",
    )(place, reduced_mine, reduced_other, *top_pieces)
    top_solution = reduce_z(top_term, top_term_other)
    top_mine = gather_z(top_solution.astype(BF))
    top_other = swap_core(top_mine)
    leaf_solution = pl.pallas_call(
        backward_kernel,
        out_shape=jax.ShapeDtypeStruct((4, 512, 256), F32),
        in_specs=[SMEM] + [VMEM] * 5,
        out_specs=VMEM,
        scratch_shapes=[pltpu.VMEM((4096, 256), F32), pltpu.VMEM((1024, 256), F32)],
        compiler_params=PARAMS,
        cost_estimate=pl.CostEstimate(flops=2 * 10**9, bytes_accessed=12 * 2**20, transcendentals=0),
        name="leaf_backward",
    )(pick_rows, inv, panel, forward, top_mine, top_other)
    return leaf_solution, top_solution


def solution(mesh):
    return jax.shard_map(
        per_device,
        mesh=mesh,
        in_specs=(
            P("snode", "rhs", None),
            P("snode", "rhs", None),
            P("snode", None),
            P("snode", None, "rhs"),
            P("snode", "rhs"),
            P("snode", "rhs"),
        ),
        out_specs=(P("snode", None, "rhs"), P("snode", "rhs")),
        check_vma=False,
    )
```

```python
import jax
import jax.numpy as jnp
from jax import lax
from jax.experimental import pallas as pl
from jax.experimental.pallas import tpu as pltpu
from jax.sharding import PartitionSpec as P

BF = jnp.bfloat16
F32 = jnp.float32
OFFSETS = (0, 3, 1, 2)
Z_OFFSETS = (0, 7, 1, 6, 2, 5, 3, 4)
ZS, XS, YS, CORES = 8, 4, 4, 2
VMEM = pl.BlockSpec(memory_space=pltpu.VMEM)
ANY = pl.BlockSpec(memory_space=pl.ANY)
SMEM = pl.BlockSpec(memory_space=pltpu.SMEM)
PARAMS = pltpu.CompilerParams(vmem_limit_bytes=50 * 1024 * 1024)


def move_rhs(a, dx, dy):
    pairs = [(4 * x + y, 4 * ((x + dx) % 4) + (y + dy) % 4) for x in range(XS) for y in range(YS)]
    return lax.ppermute(a, "rhs", pairs)


def move_z(a, d):
    return lax.ppermute(a, "snode", [(i, (i + 2 * d) % 16) for i in range(16)])


def swap_core(a):
    return lax.ppermute(a, "snode", [(i, i ^ 1) for i in range(16)])


def around(a, move):
    return move(a, 1), move(a, -1)


def far(before, after, move):
    half = before.shape[0] // 2
    return move(before[:half], 1), move(after[half:], -1)


def along_x(a, d):
    return move_rhs(a, d, 0)


def along_y(a, d):
    return move_rhs(a, 0, d)


def gather_factors(first, second, top_inv):
    across = lax.ppermute(top_inv, ("snode", "rhs"), [(16 * a + b, 16 * b + a) for a in range(16) for b in range(16)])
    a1, b1 = around(first, along_y), around(second, along_x)
    z1 = around(top_inv, move_z)
    a1, b1, z1, across = lax.optimization_barrier((a1, b1, z1, across))
    left = lax.all_gather(across, "rhs", axis=0, tiled=True)
    near_a = jnp.concatenate([first, *a1, *far(*a1, along_y)], axis=0)
    near_b = jnp.concatenate([second, *b1, *far(*b1, along_x)], axis=0)
    a2, b2 = around(near_a, along_x), around(near_b, along_y)
    z2 = move_z(z1[0], 1), move_z(z1[1], -1)
    z3 = move_z(z2[0], 1), move_z(z2[1], -1)
    a2, b2, z3 = lax.optimization_barrier((a2, b2, z3))
    pieces = [near_a, *a2, *far(*a2, along_x), near_b, *b2, *far(*b2, along_y)]
    z4 = far(*z3, move_z)
    right = jnp.concatenate([top_inv, *z1, *z2, *z3, *z4], axis=0)
    *pieces, right = lax.optimization_barrier((*pieces, right))
    return pieces, left, right


def exchange_z(a):
    groups = [[2 * z + c for z in range(ZS)] for c in range(CORES)]
    return lax.all_to_all(a, "snode", 0, 0, axis_index_groups=groups)


def gather_z(a):
    mine = exchange_z(jnp.broadcast_to(a[None], (ZS, *a.shape)))
    return mine, swap_core(mine)


def each_block(pieces, x, y, per):
    for half in range(2):
        group = pieces[5 * half : 5 * half + 5]
        for far in range(4):
            for near in range(4):
                if far < 3:
                    piece, at = group[far], near * per
                else:
                    piece, at = (group[3], near * per) if near < 2 else (group[4], (near - 2) * per)
                a, b = (OFFSETS[far], OFFSETS[near]) if half == 0 else (OFFSETS[near], OFFSETS[far])
                yield half, piece, at, lax.rem(x + a, 4), lax.rem(y + b, 4)


def forward_kernel(place, rows, loads, *refs):
    pieces, (inv, panel, forward, update, partial_value) = refs[:10], refs[10:]
    x, y = place[2], place[3]
    for half, piece, at, bx, by in each_block(pieces, x, y, 2):
        r = 4 * bx + by
        for leaf in range(2):
            inv[2 * half + leaf, pl.ds(pl.multiple_of(r * 32, 32), 32), :] = piece[at + leaf, :32, :]
            panel[2 * half + leaf, pl.ds(pl.multiple_of(r * 64, 64), 64), :] = piece[at + leaf, 32:, :]
    for leaf in range(4):
        value = jnp.dot(inv[leaf], loads[leaf], preferred_element_type=F32).astype(BF)
        forward[leaf] = value
        partial_value[leaf * 1024 : leaf * 1024 + 1024, :] = jnp.dot(
            panel[leaf], value, preferred_element_type=F32
        ).astype(BF)

    @pl.loop(0, 4)
    def _(block):
        total = None
        for k in range(8):
            target = rows[0:1, k * 512 : k * 512 + 512] - block * 1024
            hit = lax.broadcasted_iota(jnp.int32, (1024, 512), 0) == target
            term = jnp.dot(
                hit.astype(F32).astype(BF), partial_value[k * 512 : k * 512 + 512, :], preferred_element_type=F32
            )
            total = term if total is None else total + term
        update[pl.ds(pl.multiple_of(block * 1024, 1024), 1024), :] = total.astype(BF)


def square_kernel(place, after, left, right, right_other, out, total):
    z, c = place[0], place[1]
    for k, offset in enumerate(Z_OFFSETS):
        chip = lax.rem(z + offset, 8)
        for core, part in ((c, right), (1 - c, right_other)):
            first = pl.multiple_of((2 * chip + core) * 256, 256)
            total[pl.ds(first, 256), :] = part[k * 256 : k * 256 + 256, :]
    out[...] = lax.dot_general(
        left[...], total[...], (((0,), (0,)), ((), ())), preferred_element_type=F32
    ).astype(BF)


def top_kernel(place, reduced_mine, reduced_other, square, out, row_block, reduced):
    c = place[1]
    for k in range(16):
        row_block[:, k * 256 : k * 256 + 256] = square[k * 256 : k * 256 + 256, :]
    for k in range(8):
        reduced[pl.ds(pl.multiple_of((2 * k + c) * 256, 256), 256), :] = reduced_mine[k]
        reduced[pl.ds(pl.multiple_of((2 * k + 1 - c) * 256, 256), 256), :] = reduced_other[k]
    out[...] = jnp.dot(row_block[...], reduced[...], preferred_element_type=F32)


def backward_kernel(rows, inv, panel, forward, top_mine, top_other, out, top, picked):
    for k in range(8):
        top[k * 256 : k * 256 + 256, :] = top_mine[k].astype(F32)
        top[2048 + k * 256 : 2048 + k * 256 + 256, :] = top_other[k].astype(F32)
    for leaf in range(4):

        @pl.loop(0, 1024 // 16)
        def _(step):
            first = pl.multiple_of(step * 16, 16)
            found = [top[pl.ds(rows[leaf * 1024 + first + k], 1), :] for k in range(16)]
            picked[pl.ds(first, 16), :] = jnp.concatenate(found, axis=0).astype(BF)

        through = lax.dot_general(panel[leaf], picked[...], (((0,), (0,)), ((), ())), preferred_element_type=F32)
        value = (forward[leaf].astype(F32) - through).astype(BF)
        out[leaf] = lax.dot_general(inv[leaf], value, (((0,), (0,)), ((), ())), preferred_element_type=F32)


def per_device(leaf_inv, leaf_panel, leaf_rows, leaf_loads, top_inv, top_loads):
    s, r = lax.axis_index("snode"), lax.axis_index("rhs")
    z, c, x, y = s // 2, s % 2, r // 4, r % 4
    place = jnp.stack([z, c, x, y]).astype(jnp.int32)
    own_core = ((leaf_rows // 256) % 2) == c
    slots = (jnp.where(own_core, 0, 2048) + (leaf_rows // 512) * 256 + leaf_rows % 256).reshape(-1)

    factors = jnp.concatenate([leaf_inv, leaf_panel], axis=1)
    pieces, left, right = gather_factors(factors[:2], factors[2:], top_inv)
    right_other = swap_core(right)
    inv, panel, forward, update = pl.pallas_call(
        forward_kernel,
        out_shape=(
            jax.ShapeDtypeStruct((4, 512, 512), BF),
            jax.ShapeDtypeStruct((4, 1024, 512), BF),
            jax.ShapeDtypeStruct((4, 512, 256), BF),
            jax.ShapeDtypeStruct((4096, 256), BF),
        ),
        in_specs=[SMEM] + [VMEM] * 12,
        out_specs=[VMEM] * 4,
        scratch_shapes=[pltpu.VMEM((4096, 256), BF)],
        compiler_params=PARAMS,
        cost_estimate=pl.CostEstimate(flops=10**10, bytes_accessed=20 * 2**20, transcendentals=0),
        name="leaf_forward",
    )(place, jnp.broadcast_to(slots[None], (8, 4096)), leaf_loads, *pieces)

    square = pl.pallas_call(
        square_kernel,
        out_shape=jax.ShapeDtypeStruct((256, 256), BF),
        in_specs=[SMEM, ANY] + [VMEM] * 3,
        out_specs=VMEM,
        scratch_shapes=[pltpu.VMEM((4096, 256), BF)],
        compiler_params=PARAMS,
        cost_estimate=pl.CostEstimate(flops=10**9, bytes_accessed=6 * 2**20, transcendentals=0),
        name="top_square",
    )(place, forward, left, right, right_other)
    square_rows = lax.all_gather(square, "rhs", axis=0, tiled=True)

    update = update.reshape(2, 8, 256, 256)
    chip = (update[0].astype(F32) + swap_core(update[1]).astype(F32)).astype(BF)
    total = jnp.sum(exchange_z(chip).astype(F32), axis=0)
    reduced = (top_loads.astype(F32) - total).astype(BF)
    reduced_mine, reduced_other = gather_z(reduced)
    top_solution = pl.pallas_call(
        top_kernel,
        out_shape=jax.ShapeDtypeStruct((256, 256), F32),
        in_specs=[SMEM] + [VMEM] * 3,
        out_specs=VMEM,
        scratch_shapes=[pltpu.VMEM((256, 4096), BF), pltpu.VMEM((4096, 256), BF)],
        compiler_params=PARAMS,
        cost_estimate=pl.CostEstimate(flops=10**9, bytes_accessed=6 * 2**20, transcendentals=0),
        name="top_solve",
    )(place, reduced_mine, reduced_other, square_rows)
    top_mine, top_other = gather_z(top_solution.astype(BF))
    leaf_solution = pl.pallas_call(
        backward_kernel,
        out_shape=jax.ShapeDtypeStruct((4, 512, 256), F32),
        in_specs=[SMEM] + [VMEM] * 5,
        out_specs=VMEM,
        scratch_shapes=[pltpu.VMEM((4096, 256), F32), pltpu.VMEM((1024, 256), BF)],
        compiler_params=PARAMS,
        cost_estimate=pl.CostEstimate(flops=10**10, bytes_accessed=12 * 2**20, transcendentals=0),
        name="leaf_backward",
    )(slots, inv, panel, forward, top_mine, top_other)
    return leaf_solution, top_solution


def solution(mesh):
    return jax.shard_map(
        per_device,
        mesh=mesh,
        in_specs=(
            P("snode", "rhs", None),
            P("snode", "rhs", None),
            P("snode", None),
            P("snode", None, "rhs"),
            P("snode", "rhs"),
            P("snode", "rhs"),
        ),
        out_specs=(P("snode", None, "rhs"), P("snode", "rhs")),
        check_vma=False,
    )
```

```python
import jax
import jax.numpy as jnp
from jax import lax
from jax.experimental import pallas as pl
from jax.experimental.pallas import tpu as pltpu
from jax.sharding import PartitionSpec as P

BF = jnp.bfloat16
F32 = jnp.float32
OFFSETS = (0, 3, 1, 2)
XS, YS = 4, 4
Z_GROUPS = [[2 * z + c for z in range(8)] for c in range(2)]
VMEM = pl.BlockSpec(memory_space=pltpu.VMEM)
ANY = pl.BlockSpec(memory_space=pl.ANY)
SMEM = pl.BlockSpec(memory_space=pltpu.SMEM)
PARAMS = pltpu.CompilerParams(vmem_limit_bytes=50 * 1024 * 1024)


def move_rhs(a, dx, dy):
    pairs = [(4 * x + y, 4 * ((x + dx) % 4) + (y + dy) % 4) for x in range(XS) for y in range(YS)]
    return lax.ppermute(a, "rhs", pairs)


def swap_core(a):
    return lax.ppermute(a, "snode", [(i, i ^ 1) for i in range(16)])


def around(a, move):
    return move(a, 1), move(a, -1)


def far(before, after, move):
    half = before.shape[0] // 2
    return move(before[:half], 1), move(after[half:], -1)


def along_x(a, d):
    return move_rhs(a, d, 0)


def along_y(a, d):
    return move_rhs(a, 0, d)


def gather_factors(first, second, top_inv):
    across = lax.ppermute(top_inv, ("snode", "rhs"), [(16 * a + b, 16 * b + a) for a in range(16) for b in range(16)])
    a1, b1 = around(first, along_y), around(second, along_x)
    near_a = jnp.concatenate([first, *a1, *far(*a1, along_y)], axis=0)
    near_b = jnp.concatenate([second, *b1, *far(*b1, along_x)], axis=0)
    near_a, near_b, across = lax.optimization_barrier((near_a, near_b, across))
    a2, b2 = around(near_a, along_x), around(near_b, along_y)
    return [near_a, *a2, *far(*a2, along_x), near_b, *b2, *far(*b2, along_y)], across


def exchange_z(a):
    return lax.all_to_all(a, "snode", 0, 0, axis_index_groups=Z_GROUPS)


def gather_z(a):
    def onward(b, d):
        pairs = [(i, (i + 2 * d) % 16 if i % 2 == 0 else (i - 2 * d) % 16) for i in range(16)]
        return lax.ppermute(b, "snode", pairs)

    rows = a.shape[0]
    chip = jnp.concatenate([a, swap_core(a)], axis=0)
    second = onward(chip, 2)
    first = onward(chip, 1)
    third = onward(second, 1)
    fourth = onward(second[:rows], 2)
    side = jnp.concatenate([first, second, third, fourth], axis=0)
    return chip, side, swap_core(side)


def gathered_blocks(z, c):
    up = 1 - 2 * c
    yield 0, 0, z, c
    yield 0, 256, z, 1 - c
    for d in (1, 2, 3):
        below, above = lax.rem(z - d * up + 8, 8), lax.rem(z + d * up + 8, 8)
        yield 1, (d - 1) * 512, below, c
        yield 1, (d - 1) * 512 + 256, below, 1 - c
        yield 2, (d - 1) * 512, above, 1 - c
        yield 2, (d - 1) * 512 + 256, above, c
    yield 1, 1536, lax.rem(z + 4, 8), c
    yield 2, 1536, lax.rem(z + 4, 8), 1 - c


def gathered_slot(chip, own_core, z, c):
    ahead = jnp.where(c == 0, chip - z, z - chip) % 8
    own, away = jnp.where(own_core, 0, 256), jnp.where(own_core, 256, 0)
    middle = jnp.where(own_core, 512 + 1536, 2304 + 1536)
    slot = jnp.where(ahead < 4, 2304 + (ahead - 1) * 512 + away, 512 + (7 - ahead) * 512 + own)
    return jnp.where(ahead == 0, own, jnp.where(ahead == 4, middle, slot))


def each_block(pieces, x, y, per):
    for half in range(2):
        group = pieces[5 * half : 5 * half + 5]
        for far in range(4):
            for near in range(4):
                if far < 3:
                    piece, at = group[far], near * per
                else:
                    piece, at = (group[3], near * per) if near < 2 else (group[4], (near - 2) * per)
                a, b = (OFFSETS[far], OFFSETS[near]) if half == 0 else (OFFSETS[near], OFFSETS[far])
                yield half, piece, at, lax.rem(x + a, 4), lax.rem(y + b, 4)


def forward_kernel(place, rows, loads, *refs):
    pieces, (inv, panel, forward, update, partial_value) = refs[:10], refs[10:]
    x, y = place[2], place[3]
    for half, piece, at, bx, by in each_block(pieces, x, y, 2):
        r = 4 * bx + by
        for leaf in range(2):
            inv[2 * half + leaf, pl.ds(pl.multiple_of(r * 32, 32), 32), :] = piece[at + leaf, :32, :]
            panel[2 * half + leaf, pl.ds(pl.multiple_of(r * 64, 64), 64), :] = piece[at + leaf, 32:, :]
    for leaf in range(4):
        value = jnp.dot(inv[leaf], loads[leaf], preferred_element_type=F32).astype(BF)
        forward[leaf] = value
        partial_value[leaf * 1024 : leaf * 1024 + 1024, :] = jnp.dot(
            panel[leaf], value, preferred_element_type=F32
        ).astype(BF)

    @pl.loop(0, 4)
    def _(block):
        total = None
        for k in range(8):
            target = rows[0:1, k * 512 : k * 512 + 512] - block * 1024
            hit = lax.broadcasted_iota(jnp.int32, (1024, 512), 0) == target
            term = jnp.dot(
                hit.astype(F32).astype(BF), partial_value[k * 512 : k * 512 + 512, :], preferred_element_type=F32
            )
            total = term if total is None else total + term
        update[pl.ds(pl.multiple_of(block * 1024, 1024), 1024), :] = total.astype(BF)


def square_kernel(place, after, left, right, right_other, out, total):
    c = place[1]
    for chip in range(8):
        for core, part in ((c, right), (1 - c, right_other)):
            first = pl.multiple_of((2 * chip + core) * 256, 256)
            total[pl.ds(first, 256), :] = part[chip * 256 : chip * 256 + 256, :]
    out[...] = lax.dot_general(
        left[...], total[...], (((0,), (0,)), ((), ())), preferred_element_type=F32
    ).astype(BF)


def top_kernel(place, own_chip, side, side_other, square, out, row_block, reduced):
    z, c = place[0], place[1]
    for k in range(16):
        row_block[:, k * 256 : k * 256 + 256] = square[k * 256 : k * 256 + 256, :]
    pieces = (own_chip, side, side_other)
    for piece, at, chip, core in gathered_blocks(z, c):
        first = pl.multiple_of((2 * chip + core) * 256, 256)
        reduced[pl.ds(first, 256), :] = pieces[piece][at : at + 256, :]
    out[...] = jnp.dot(row_block[...], reduced[...], preferred_element_type=F32)


def backward_kernel(rows, inv, panel, forward, own_chip, side, side_other, out, top, picked):
    top[:512, :] = own_chip[...].astype(F32)
    top[512:2304, :] = side[...].astype(F32)
    top[2304:, :] = side_other[...].astype(F32)
    for leaf in range(4):

        @pl.loop(0, 1024 // 16)
        def _(step):
            first = pl.multiple_of(step * 16, 16)
            found = [top[pl.ds(rows[leaf * 1024 + first + k], 1), :] for k in range(16)]
            picked[pl.ds(first, 16), :] = jnp.concatenate(found, axis=0).astype(BF)

        through = lax.dot_general(panel[leaf], picked[...], (((0,), (0,)), ((), ())), preferred_element_type=F32)
        value = (forward[leaf].astype(F32) - through).astype(BF)
        out[leaf] = lax.dot_general(inv[leaf], value, (((0,), (0,)), ((), ())), preferred_element_type=F32)


def per_device(leaf_inv, leaf_panel, leaf_rows, leaf_loads, top_inv, top_loads):
    s, r = lax.axis_index("snode"), lax.axis_index("rhs")
    z, c, x, y = s // 2, s % 2, r // 4, r % 4
    place = jnp.stack([z, c, x, y]).astype(jnp.int32)
    own_core = ((leaf_rows // 256) % 2) == c
    chips, within = leaf_rows // 512, leaf_rows % 256
    slots = (jnp.where(own_core, 0, 2048) + chips * 256 + within).reshape(-1)
    picks = (gathered_slot(chips, own_core, z, c) + within).reshape(-1)

    factors = jnp.concatenate([leaf_inv, leaf_panel], axis=1)
    right = lax.all_gather(top_inv, "snode", axis=0, tiled=True, axis_index_groups=Z_GROUPS)
    pieces, across = gather_factors(factors[:2], factors[2:], top_inv)
    left = lax.all_gather(across, "rhs", axis=0, tiled=True)
    right_other = swap_core(right)
    inv, panel, forward, update = pl.pallas_call(
        forward_kernel,
        out_shape=(
            jax.ShapeDtypeStruct((4, 512, 512), BF),
            jax.ShapeDtypeStruct((4, 1024, 512), BF),
            jax.ShapeDtypeStruct((4, 512, 256), BF),
            jax.ShapeDtypeStruct((4096, 256), BF),
        ),
        in_specs=[SMEM] + [VMEM] * 12,
        out_specs=[VMEM] * 4,
        scratch_shapes=[pltpu.VMEM((4096, 256), BF)],
        compiler_params=PARAMS,
        cost_estimate=pl.CostEstimate(flops=10**10, bytes_accessed=20 * 2**20, transcendentals=0),
        name="leaf_forward",
    )(place, jnp.broadcast_to(slots[None], (8, 4096)), leaf_loads, *pieces)

    square = pl.pallas_call(
        square_kernel,
        out_shape=jax.ShapeDtypeStruct((256, 256), BF),
        in_specs=[SMEM, ANY] + [VMEM] * 3,
        out_specs=VMEM,
        scratch_shapes=[pltpu.VMEM((4096, 256), BF)],
        compiler_params=PARAMS,
        cost_estimate=pl.CostEstimate(flops=10**9, bytes_accessed=6 * 2**20, transcendentals=0),
        name="top_square",
    )(place, forward, left, right, right_other)
    square_rows = lax.all_gather(square, "rhs", axis=0, tiled=True)

    update = update.reshape(2, 8, 256, 256)
    chip = (update[0].astype(F32) + swap_core(update[1]).astype(F32)).astype(BF)
    total = jnp.sum(exchange_z(chip).astype(F32), axis=0)
    reduced = (top_loads.astype(F32) - total).astype(BF)
    reduced_pieces = gather_z(reduced)
    top_solution = pl.pallas_call(
        top_kernel,
        out_shape=jax.ShapeDtypeStruct((256, 256), F32),
        in_specs=[SMEM] + [VMEM] * 4,
        out_specs=VMEM,
        scratch_shapes=[pltpu.VMEM((256, 4096), BF), pltpu.VMEM((4096, 256), BF)],
        compiler_params=PARAMS,
        cost_estimate=pl.CostEstimate(flops=10**9, bytes_accessed=6 * 2**20, transcendentals=0),
        name="top_solve",
    )(place, *reduced_pieces, square_rows)
    top_pieces = gather_z(top_solution.astype(BF))
    leaf_solution = pl.pallas_call(
        backward_kernel,
        out_shape=jax.ShapeDtypeStruct((4, 512, 256), F32),
        in_specs=[SMEM] + [VMEM] * 6,
        out_specs=VMEM,
        scratch_shapes=[pltpu.VMEM((4096, 256), F32), pltpu.VMEM((1024, 256), BF)],
        compiler_params=PARAMS,
        cost_estimate=pl.CostEstimate(flops=10**10, bytes_accessed=12 * 2**20, transcendentals=0),
        name="leaf_backward",
    )(picks, inv, panel, forward, *top_pieces)
    return leaf_solution, top_solution


def solution(mesh):
    return jax.shard_map(
        per_device,
        mesh=mesh,
        in_specs=(
            P("snode", "rhs", None),
            P("snode", "rhs", None),
            P("snode", None),
            P("snode", None, "rhs"),
            P("snode", "rhs"),
            P("snode", "rhs"),
        ),
        out_specs=(P("snode", None, "rhs"), P("snode", "rhs")),
        check_vma=False,
    )
```

```python
import jax
import jax.numpy as jnp
from jax import lax
from jax.experimental import pallas as pl
from jax.experimental.pallas import tpu as pltpu
from jax.sharding import PartitionSpec as P

BF = jnp.bfloat16
F32 = jnp.float32
OFFSETS = (0, 3, 1, 2)
XS, YS = 4, 4
Z_GROUPS = [[2 * z + c for z in range(8)] for c in range(2)]
VMEM = pl.BlockSpec(memory_space=pltpu.VMEM)
ANY = pl.BlockSpec(memory_space=pl.ANY)
SMEM = pl.BlockSpec(memory_space=pltpu.SMEM)
PARAMS = pltpu.CompilerParams(vmem_limit_bytes=50 * 1024 * 1024)


def move_rhs(a, dx, dy):
    pairs = [(4 * x + y, 4 * ((x + dx) % 4) + (y + dy) % 4) for x in range(XS) for y in range(YS)]
    return lax.ppermute(a, "rhs", pairs)


def swap_core(a):
    return lax.ppermute(a, "snode", [(i, i ^ 1) for i in range(16)])


def around(a, move):
    return move(a, 1), move(a, -1)


def far(before, after, move):
    half = before.shape[0] // 2
    return move(before[:half], 1), move(after[half:], -1)


def along_x(a, d):
    return move_rhs(a, d, 0)


def along_y(a, d):
    return move_rhs(a, 0, d)


def gather_factors(first, second, top_inv):
    across = lax.ppermute(top_inv, ("snode", "rhs"), [(16 * a + b, 16 * b + a) for a in range(16) for b in range(16)])
    chip = both_cores(top_inv)
    a1, b1 = around(first, along_y), around(second, along_x)
    near_a, near_b = jnp.concatenate([first, a1[0]]), jnp.concatenate([second, b1[0]])
    a2, b2 = around(near_a, along_x), around(near_b, along_y)
    rest_a = jnp.concatenate([a1[1], *far(*a1, along_y)])
    rest_b = jnp.concatenate([b1[1], *far(*b1, along_x)])
    rest_a, rest_b, across, chip = lax.optimization_barrier((rest_a, rest_b, across, chip))
    a3, b3 = around(rest_a, along_x), around(rest_b, along_y)
    side = one_side(chip)
    last_a = along_x(a2[0], 1), along_x(a3[1], -1)
    last_b = along_y(b2[0], 1), along_y(b3[1], -1)
    pieces = [near_a, rest_a, a2[0], a3[0], a2[1], a3[1], *last_a, near_b, rest_b, b2[0], b3[0], b2[1], b3[1], *last_b]
    *pieces, side = lax.optimization_barrier((*pieces, side))
    return pieces, across, (chip, side, swap_core(side))


def exchange_z(a):
    return lax.all_to_all(a, "snode", 0, 0, axis_index_groups=Z_GROUPS)


def both_cores(a):
    return jnp.concatenate([a, swap_core(a)], axis=0)


def one_side(chip):
    def onward(b, d):
        pairs = [(i, (i + 2 * d) % 16 if i % 2 == 0 else (i - 2 * d) % 16) for i in range(16)]
        return lax.ppermute(b, "snode", pairs)

    second = onward(chip, 2)
    first = onward(chip, 1)
    third = onward(second, 1)
    fourth = onward(second[: chip.shape[0] // 2], 2)
    return jnp.concatenate([first, second, third, fourth], axis=0)


def gather_z(a):
    chip = both_cores(a)
    side = one_side(chip)
    return chip, side, swap_core(side)


def gathered_blocks(z, c):
    up = 1 - 2 * c
    yield 0, 0, z, c
    yield 0, 256, z, 1 - c
    for d in (1, 2, 3):
        below, above = lax.rem(z - d * up + 8, 8), lax.rem(z + d * up + 8, 8)
        yield 1, (d - 1) * 512, below, c
        yield 1, (d - 1) * 512 + 256, below, 1 - c
        yield 2, (d - 1) * 512, above, 1 - c
        yield 2, (d - 1) * 512 + 256, above, c
    yield 1, 1536, lax.rem(z + 4, 8), c
    yield 2, 1536, lax.rem(z + 4, 8), 1 - c


def gathered_slot(chip, own_core, z, c):
    ahead = jnp.where(c == 0, chip - z, z - chip) % 8
    own, away = jnp.where(own_core, 0, 256), jnp.where(own_core, 256, 0)
    middle = jnp.where(own_core, 512 + 1536, 2304 + 1536)
    slot = jnp.where(ahead < 4, 2304 + (ahead - 1) * 512 + away, 512 + (7 - ahead) * 512 + own)
    return jnp.where(ahead == 0, own, jnp.where(ahead == 4, middle, slot))


def each_block(pieces, x, y):
    for half in range(2):
        for far_at in range(4):
            for near_at in range(4):
                piece = pieces[8 * half + 2 * far_at + near_at // 2]
                a, b = OFFSETS[far_at], OFFSETS[near_at]
                a, b = (a, b) if half == 0 else (b, a)
                yield half, piece, near_at % 2 * 2, lax.rem(x + a, 4), lax.rem(y + b, 4)


def place_rows(rows, values, out, base):
    @pl.loop(0, 2)
    def _(block):
        total = None
        for k in range(8):
            target = rows[0:1, k * 512 : k * 512 + 512] - (block * 1024 + base)
            hit = lax.broadcasted_iota(jnp.int32, (1024, 512), 0) == target
            term = jnp.dot(
                hit.astype(F32).astype(BF), values[k * 512 : k * 512 + 512, :], preferred_element_type=F32
            )
            total = term if total is None else total + term
        out[pl.ds(pl.multiple_of(block * 1024, 1024), 1024), :] = total.astype(BF)


def forward_kernel(place, rows, loads, *refs):
    pieces, (inv, panel, forward, mine, other, partial_value) = refs[:16], refs[16:]
    x, y = place[2], place[3]
    for half, piece, at, bx, by in each_block(pieces, x, y):
        r = 4 * bx + by
        for leaf in range(2):
            inv[2 * half + leaf, pl.ds(pl.multiple_of(r * 32, 32), 32), :] = piece[at + leaf, :32, :]
            panel[2 * half + leaf, pl.ds(pl.multiple_of(r * 64, 64), 64), :] = piece[at + leaf, 32:, :]
    for leaf in range(4):
        value = jnp.dot(inv[leaf], loads[leaf], preferred_element_type=F32).astype(BF)
        forward[leaf] = value
        partial_value[leaf * 1024 : leaf * 1024 + 1024, :] = jnp.dot(
            panel[leaf], value, preferred_element_type=F32
        ).astype(BF)
    place_rows(rows, partial_value, other, 2048)
    place_rows(rows, partial_value, mine, 0)


def turn_kernel(inv, panel, inv_t, panel_t):
    for leaf in range(4):
        inv_t[leaf] = inv[leaf].T
        panel_t[leaf] = panel[leaf].T


def square_kernel(place, after, left, own_chip, side, side_other, out, total):
    gathered_rows(place, (own_chip, side, side_other), total)
    out[...] = lax.dot_general(
        left[...], total[...], (((0,), (0,)), ((), ())), preferred_element_type=F32
    ).astype(BF)


def gathered_rows(place, pieces, out):
    for piece, at, chip, core in gathered_blocks(place[0], place[1]):
        first = pl.multiple_of((2 * chip + core) * 256, 256)
        out[pl.ds(first, 256), :] = pieces[piece][at : at + 256, :]


def top_kernel(place, own_chip, side, side_other, square, out, rounded, row_block, reduced):
    for k in range(16):
        row_block[:, k * 256 : k * 256 + 256] = square[k * 256 : k * 256 + 256, :]
    gathered_rows(place, (own_chip, side, side_other), reduced)
    value = jnp.dot(row_block[...], reduced[...], preferred_element_type=F32)
    out[...] = value
    rounded[...] = value.astype(BF)


def backward_kernel(rows, inv_t, panel_t, forward, own_chip, side, side_other, out, top, picked):
    top[:512, :] = own_chip[...].astype(F32)
    top[512:2304, :] = side[...].astype(F32)
    top[2304:, :] = side_other[...].astype(F32)
    for leaf in range(4):

        @pl.loop(0, 1024 // 16)
        def _(step):
            first = pl.multiple_of(step * 16, 16)
            found = [top[pl.ds(rows[leaf * 1024 + first + k], 1), :] for k in range(16)]
            picked[pl.ds(first, 16), :] = jnp.concatenate(found, axis=0).astype(BF)

        through = jnp.dot(panel_t[leaf], picked[...], preferred_element_type=F32)
        value = (forward[leaf].astype(F32) - through).astype(BF)
        out[leaf] = jnp.dot(inv_t[leaf], value, preferred_element_type=F32)


def per_device(leaf_inv, leaf_panel, leaf_rows, leaf_loads, top_inv, top_loads):
    s, r = lax.axis_index("snode"), lax.axis_index("rhs")
    z, c, x, y = s // 2, s % 2, r // 4, r % 4
    place = jnp.stack([z, c, x, y]).astype(jnp.int32)
    own_core = ((leaf_rows // 256) % 2) == c
    chips, within = leaf_rows // 512, leaf_rows % 256
    slots = (jnp.where(own_core, 0, 2048) + chips * 256 + within).reshape(-1)
    picks = (gathered_slot(chips, own_core, z, c) + within).reshape(-1)

    factors = jnp.concatenate([leaf_inv, leaf_panel], axis=1)
    pieces, across, right = gather_factors(factors[:2], factors[2:], top_inv)
    left = lax.all_gather(across, "rhs", axis=0, tiled=True)
    inv, panel, forward, mine, other = pl.pallas_call(
        forward_kernel,
        out_shape=(
            jax.ShapeDtypeStruct((4, 512, 512), BF),
            jax.ShapeDtypeStruct((4, 1024, 512), BF),
            jax.ShapeDtypeStruct((4, 512, 256), BF),
            jax.ShapeDtypeStruct((2048, 256), BF),
            jax.ShapeDtypeStruct((2048, 256), BF),
        ),
        in_specs=[SMEM] + [VMEM] * 18,
        out_specs=[VMEM] * 5,
        scratch_shapes=[pltpu.VMEM((4096, 256), BF)],
        compiler_params=PARAMS,
        cost_estimate=pl.CostEstimate(flops=10**10, bytes_accessed=20 * 2**20, transcendentals=0),
        name="leaf_forward",
    )(place, jnp.broadcast_to(slots[None], (8, 4096)), leaf_loads, *pieces)

    square = pl.pallas_call(
        square_kernel,
        out_shape=jax.ShapeDtypeStruct((256, 256), BF),
        in_specs=[SMEM, ANY] + [VMEM] * 4,
        out_specs=VMEM,
        scratch_shapes=[pltpu.VMEM((4096, 256), BF)],
        compiler_params=PARAMS,
        cost_estimate=pl.CostEstimate(flops=10**9, bytes_accessed=6 * 2**20, transcendentals=0),
        name="top_square",
    )(place, forward, left, *right)
    square_rows = lax.all_gather(square, "rhs", axis=0, tiled=True)
    inv_t, panel_t = pl.pallas_call(
        turn_kernel,
        out_shape=(jax.ShapeDtypeStruct((4, 512, 512), BF), jax.ShapeDtypeStruct((4, 512, 1024), BF)),
        in_specs=[VMEM] * 2,
        out_specs=[VMEM] * 2,
        compiler_params=PARAMS,
        cost_estimate=pl.CostEstimate(flops=0, bytes_accessed=12 * 2**20, transcendentals=0),
        name="leaf_turn",
    )(inv, panel)

    chip = (mine.astype(F32) + swap_core(other).astype(F32)).astype(BF).reshape(8, 256, 256)
    parts, inv_t, panel_t = lax.optimization_barrier((exchange_z(chip), inv_t, panel_t))
    total = jnp.sum(parts.astype(F32), axis=0)
    reduced = (top_loads.astype(F32) - total).astype(BF)
    top_solution, top_rounded = pl.pallas_call(
        top_kernel,
        out_shape=(jax.ShapeDtypeStruct((256, 256), F32), jax.ShapeDtypeStruct((256, 256), BF)),
        in_specs=[SMEM] + [VMEM] * 4,
        out_specs=[VMEM] * 2,
        scratch_shapes=[pltpu.VMEM((256, 4096), BF), pltpu.VMEM((4096, 256), BF)],
        compiler_params=PARAMS,
        cost_estimate=pl.CostEstimate(flops=10**9, bytes_accessed=6 * 2**20, transcendentals=0),
        name="top_solve",
    )(place, *gather_z(reduced), square_rows)
    leaf_solution = pl.pallas_call(
        backward_kernel,
        out_shape=jax.ShapeDtypeStruct((4, 512, 256), F32),
        in_specs=[SMEM] + [VMEM] * 6,
        out_specs=VMEM,
        scratch_shapes=[pltpu.VMEM((4096, 256), F32), pltpu.VMEM((1024, 256), BF)],
        compiler_params=PARAMS,
        cost_estimate=pl.CostEstimate(flops=10**10, bytes_accessed=12 * 2**20, transcendentals=0),
        name="leaf_backward",
    )(picks, inv_t, panel_t, forward, *gather_z(top_rounded))
    return leaf_solution, top_solution


def solution(mesh):
    return jax.shard_map(
        per_device,
        mesh=mesh,
        in_specs=(
            P("snode", "rhs", None),
            P("snode", "rhs", None),
            P("snode", None),
            P("snode", None, "rhs"),
            P("snode", "rhs"),
            P("snode", "rhs"),
        ),
        out_specs=(P("snode", None, "rhs"), P("snode", "rhs")),
        check_vma=False,
    )
```

```python
import jax
import jax.numpy as jnp
from jax import lax
from jax.experimental import pallas as pl
from jax.experimental.pallas import tpu as pltpu
from jax.sharding import PartitionSpec as P

BF = jnp.bfloat16
F32 = jnp.float32
OFFSETS = (0, 3, 1, 2)
XS, YS = 4, 4
Z_GROUPS = [[2 * z + c for z in range(8)] for c in range(2)]
VMEM = pl.BlockSpec(memory_space=pltpu.VMEM)
ANY = pl.BlockSpec(memory_space=pl.ANY)
SMEM = pl.BlockSpec(memory_space=pltpu.SMEM)
PARAMS = pltpu.CompilerParams(vmem_limit_bytes=50 * 1024 * 1024)


def move_rhs(a, dx, dy):
    pairs = [(4 * x + y, 4 * ((x + dx) % 4) + (y + dy) % 4) for x in range(XS) for y in range(YS)]
    return lax.ppermute(a, "rhs", pairs)


def swap_core(a):
    return lax.ppermute(a, "snode", [(i, i ^ 1) for i in range(16)])


def around(a, move):
    return move(a, 1), move(a, -1)


def far(before, after, move):
    half = before.shape[0] // 2
    return move(before[:half], 1), move(after[half:], -1)


def along_x(a, d):
    return move_rhs(a, d, 0)


def along_y(a, d):
    return move_rhs(a, 0, d)


def gather_factors(first, second, top_inv):
    across = lax.ppermute(top_inv, ("snode", "rhs"), [(16 * a + b, 16 * b + a) for a in range(16) for b in range(16)])
    a1, b1 = around(first, along_y), around(second, along_x)
    near_a = jnp.concatenate([first, *a1, *far(*a1, along_y)], axis=0)
    near_b = jnp.concatenate([second, *b1, *far(*b1, along_x)], axis=0)
    near_a, near_b, across, top_inv = lax.optimization_barrier((near_a, near_b, across, top_inv))
    a2, b2 = around(near_a, along_x), around(near_b, along_y)
    right = exchange_z(jnp.broadcast_to(top_inv[None], (8, *top_inv.shape)))
    pieces = [near_a, *a2, *far(*a2, along_x), near_b, *b2, *far(*b2, along_y)]
    *pieces, right = lax.optimization_barrier((*pieces, right))
    return pieces, across, right.reshape(2048, 256)


def exchange_z(a):
    return lax.all_to_all(a, "snode", 0, 0, axis_index_groups=Z_GROUPS)


def onward(a, d):
    return lax.ppermute(a, "snode", [(i, (i + 2 * d) % 16 if i % 2 == 0 else (i - 2 * d) % 16) for i in range(16)])


def sum_slot(chip, own_core, z, c):
    ahead = jnp.where(c == 0, chip - z, z - chip) % 8
    keep = jnp.where(ahead % 4 == 0, own_core, ahead < 4)
    distance = jnp.where(ahead < 4, ahead, 8 - ahead)
    second = jnp.where(keep == own_core, 0, 256)
    slot = jnp.where(distance == 0, 0, jnp.where(distance == 4, 1792, distance * 512 - 256 + second))
    return jnp.where(keep, slot, 2048 + slot)


def sum_z(keep, give):
    chip = keep.astype(F32) + swap_core(give).astype(F32)
    third, fourth, first = onward(chip[1280:1792].astype(BF), 1), onward(chip[1792:].astype(BF), 2), onward(chip[256:768].astype(BF), 1)
    second = chip[768:1280] + third.astype(F32)
    second = jnp.concatenate([second[:256] + fourth.astype(F32), second[256:]], axis=0).astype(BF)
    side = first.astype(F32) + onward(second, 2).astype(F32)
    return chip[:256] + side[:256] + swap_core(side[256:])


def gather_z(a):
    rows = a.shape[0]
    chip = jnp.concatenate([a, swap_core(a)], axis=0)
    second = onward(chip, 2)
    first = onward(chip, 1)
    third = onward(second, 1)
    fourth = onward(second[:rows], 2)
    side = jnp.concatenate([first, second, third, fourth], axis=0)
    return chip, side, swap_core(side)


def gathered_blocks(z, c):
    up = 1 - 2 * c
    yield 0, 0, z, c
    yield 0, 256, z, 1 - c
    for d in (1, 2, 3):
        below, above = lax.rem(z - d * up + 8, 8), lax.rem(z + d * up + 8, 8)
        yield 1, (d - 1) * 512, below, c
        yield 1, (d - 1) * 512 + 256, below, 1 - c
        yield 2, (d - 1) * 512, above, 1 - c
        yield 2, (d - 1) * 512 + 256, above, c
    yield 1, 1536, lax.rem(z + 4, 8), c
    yield 2, 1536, lax.rem(z + 4, 8), 1 - c


def gathered_slot(chip, own_core, z, c):
    ahead = jnp.where(c == 0, chip - z, z - chip) % 8
    own, away = jnp.where(own_core, 0, 256), jnp.where(own_core, 256, 0)
    middle = jnp.where(own_core, 512 + 1536, 2304 + 1536)
    slot = jnp.where(ahead < 4, 2304 + (ahead - 1) * 512 + away, 512 + (7 - ahead) * 512 + own)
    return jnp.where(ahead == 0, own, jnp.where(ahead == 4, middle, slot))


def each_block(pieces, x, y, per):
    for half in range(2):
        group = pieces[5 * half : 5 * half + 5]
        for far in range(4):
            for near in range(4):
                if far < 3:
                    piece, at = group[far], near * per
                else:
                    piece, at = (group[3], near * per) if near < 2 else (group[4], (near - 2) * per)
                a, b = (OFFSETS[far], OFFSETS[near]) if half == 0 else (OFFSETS[near], OFFSETS[far])
                yield half, piece, at, lax.rem(x + a, 4), lax.rem(y + b, 4)


def place_rows(rows, values, out, base):
    @pl.loop(0, 2)
    def _(block):
        total = None
        for k in range(8):
            target = rows[0:1, k * 512 : k * 512 + 512] - (block * 1024 + base)
            hit = lax.broadcasted_iota(jnp.int32, (1024, 512), 0) == target
            term = jnp.dot(
                hit.astype(F32).astype(BF), values[k * 512 : k * 512 + 512, :], preferred_element_type=F32
            )
            total = term if total is None else total + term
        out[pl.ds(pl.multiple_of(block * 1024, 1024), 1024), :] = total.astype(BF)


def forward_kernel(place, rows, loads, *refs):
    pieces, (inv, panel, forward, keep, give, partial_value) = refs[:10], refs[10:]
    x, y = place[2], place[3]
    for half, piece, at, bx, by in each_block(pieces, x, y, 2):
        r = 4 * bx + by
        for leaf in range(2):
            inv[2 * half + leaf, pl.ds(pl.multiple_of(r * 32, 32), 32), :] = piece[at + leaf, :32, :]
            panel[2 * half + leaf, pl.ds(pl.multiple_of(r * 64, 64), 64), :] = piece[at + leaf, 32:, :]
    for leaf in range(4):
        value = jnp.dot(inv[leaf], loads[leaf], preferred_element_type=F32).astype(BF)
        forward[leaf] = value
        partial_value[leaf * 1024 : leaf * 1024 + 1024, :] = jnp.dot(
            panel[leaf], value, preferred_element_type=F32
        ).astype(BF)

    place_rows(rows, partial_value, give, 2048)
    place_rows(rows, partial_value, keep, 0)


def square_kernel(place, after, left, right, right_other, out, total):
    c = place[1]
    for chip in range(8):
        for core, part in ((c, right), (1 - c, right_other)):
            first = pl.multiple_of((2 * chip + core) * 256, 256)
            total[pl.ds(first, 256), :] = part[chip * 256 : chip * 256 + 256, :]
    out[...] = lax.dot_general(
        left[...], total[...], (((0,), (0,)), ((), ())), preferred_element_type=F32
    ).astype(BF)


def top_kernel(place, own_chip, side, side_other, square, out, rounded, row_block, reduced):
    z, c = place[0], place[1]
    for k in range(16):
        row_block[:, k * 256 : k * 256 + 256] = square[k * 256 : k * 256 + 256, :]
    pieces = (own_chip, side, side_other)
    for piece, at, chip, core in gathered_blocks(z, c):
        first = pl.multiple_of((2 * chip + core) * 256, 256)
        reduced[pl.ds(first, 256), :] = pieces[piece][at : at + 256, :]
    value = jnp.dot(row_block[...], reduced[...], preferred_element_type=F32)
    out[...] = value
    rounded[...] = value.astype(BF)


def backward_kernel(rows, inv, panel, forward, own_chip, side, side_other, out, top, picked):
    top[:512, :] = own_chip[...].astype(F32)
    top[512:2304, :] = side[...].astype(F32)
    top[2304:, :] = side_other[...].astype(F32)
    for leaf in range(4):

        @pl.loop(0, 1024 // 16)
        def _(step):
            first = pl.multiple_of(step * 16, 16)
            found = [top[pl.ds(rows[leaf * 1024 + first + k], 1), :] for k in range(16)]
            picked[pl.ds(first, 16), :] = jnp.concatenate(found, axis=0).astype(BF)

        through = lax.dot_general(panel[leaf], picked[...], (((0,), (0,)), ((), ())), preferred_element_type=F32)
        value = (forward[leaf].astype(F32) - through).astype(BF)
        out[leaf] = lax.dot_general(inv[leaf], value, (((0,), (0,)), ((), ())), preferred_element_type=F32)


def per_device(leaf_inv, leaf_panel, leaf_rows, leaf_loads, top_inv, top_loads):
    s, r = lax.axis_index("snode"), lax.axis_index("rhs")
    z, c, x, y = s // 2, s % 2, r // 4, r % 4
    place = jnp.stack([z, c, x, y]).astype(jnp.int32)
    own_core = ((leaf_rows // 256) % 2) == c
    chips, within = leaf_rows // 512, leaf_rows % 256
    slots = (sum_slot(chips, own_core, z, c) + within).reshape(-1)
    picks = (gathered_slot(chips, own_core, z, c) + within).reshape(-1)

    factors = jnp.concatenate([leaf_inv, leaf_panel], axis=1)
    pieces, across, right = gather_factors(factors[:2], factors[2:], top_inv)
    left = lax.all_gather(across, "rhs", axis=0, tiled=True)
    right_other = swap_core(right)
    inv, panel, forward, keep, give = pl.pallas_call(
        forward_kernel,
        out_shape=(
            jax.ShapeDtypeStruct((4, 512, 512), BF),
            jax.ShapeDtypeStruct((4, 1024, 512), BF),
            jax.ShapeDtypeStruct((4, 512, 256), BF),
            jax.ShapeDtypeStruct((2048, 256), BF),
            jax.ShapeDtypeStruct((2048, 256), BF),
        ),
        in_specs=[SMEM] + [VMEM] * 12,
        out_specs=[VMEM] * 5,
        scratch_shapes=[pltpu.VMEM((4096, 256), BF)],
        compiler_params=PARAMS,
        cost_estimate=pl.CostEstimate(flops=10**10, bytes_accessed=20 * 2**20, transcendentals=0),
        name="leaf_forward",
    )(place, jnp.broadcast_to(slots[None], (8, 4096)), leaf_loads, *pieces)

    square = pl.pallas_call(
        square_kernel,
        out_shape=jax.ShapeDtypeStruct((256, 256), BF),
        in_specs=[SMEM, ANY] + [VMEM] * 3,
        out_specs=VMEM,
        scratch_shapes=[pltpu.VMEM((4096, 256), BF)],
        compiler_params=PARAMS,
        cost_estimate=pl.CostEstimate(flops=10**9, bytes_accessed=6 * 2**20, transcendentals=0),
        name="top_square",
    )(place, forward, left, right, right_other)
    square_rows = lax.all_gather(square, "rhs", axis=0, tiled=True)

    reduced = (top_loads.astype(F32) - sum_z(keep, give)).astype(BF)
    reduced_pieces = gather_z(reduced)
    top_solution, top_rounded = pl.pallas_call(
        top_kernel,
        out_shape=(jax.ShapeDtypeStruct((256, 256), F32), jax.ShapeDtypeStruct((256, 256), BF)),
        in_specs=[SMEM] + [VMEM] * 4,
        out_specs=[VMEM] * 2,
        scratch_shapes=[pltpu.VMEM((256, 4096), BF), pltpu.VMEM((4096, 256), BF)],
        compiler_params=PARAMS,
        cost_estimate=pl.CostEstimate(flops=10**9, bytes_accessed=6 * 2**20, transcendentals=0),
        name="top_solve",
    )(place, *reduced_pieces, square_rows)
    top_pieces = gather_z(top_rounded)
    leaf_solution = pl.pallas_call(
        backward_kernel,
        out_shape=jax.ShapeDtypeStruct((4, 512, 256), F32),
        in_specs=[SMEM] + [VMEM] * 6,
        out_specs=VMEM,
        scratch_shapes=[pltpu.VMEM((4096, 256), F32), pltpu.VMEM((1024, 256), BF)],
        compiler_params=PARAMS,
        cost_estimate=pl.CostEstimate(flops=10**10, bytes_accessed=12 * 2**20, transcendentals=0),
        name="leaf_backward",
    )(picks, inv, panel, forward, *top_pieces)
    return leaf_solution, top_solution


def solution(mesh):
    return jax.shard_map(
        per_device,
        mesh=mesh,
        in_specs=(
            P("snode", "rhs", None),
            P("snode", "rhs", None),
            P("snode", None),
            P("snode", None, "rhs"),
            P("snode", "rhs"),
            P("snode", "rhs"),
        ),
        out_specs=(P("snode", None, "rhs"), P("snode", "rhs")),
        check_vma=False,
    )
```

```python
import jax
import jax.numpy as jnp
from jax import lax
from jax.experimental import pallas as pl
from jax.experimental.pallas import tpu as pltpu
from jax.sharding import PartitionSpec as P

BF = jnp.bfloat16
F32 = jnp.float32
OFFSETS = (0, 3, 1, 2)
XS, YS = 4, 4
Z_GROUPS = [[2 * z + c for z in range(8)] for c in range(2)]
VMEM = pl.BlockSpec(memory_space=pltpu.VMEM)
ANY = pl.BlockSpec(memory_space=pl.ANY)
SMEM = pl.BlockSpec(memory_space=pltpu.SMEM)


def grant(mebibytes):
    return pltpu.CompilerParams(vmem_limit_bytes=mebibytes * 1024 * 1024)


def move_rhs(a, dx, dy):
    pairs = [(4 * x + y, 4 * ((x + dx) % 4) + (y + dy) % 4) for x in range(XS) for y in range(YS)]
    return lax.ppermute(a, "rhs", pairs)


def swap_core(a):
    return lax.ppermute(a, "snode", [(i, i ^ 1) for i in range(16)])


def around(a, move):
    return move(a, 1), move(a, -1)


def far(before, after, move):
    half = before.shape[0] // 2
    return move(before[:half], 1), move(after[half:], -1)


def along_x(a, d):
    return move_rhs(a, d, 0)


def along_y(a, d):
    return move_rhs(a, 0, d)


def gather_factors(first, second, top_inv):
    across = lax.ppermute(top_inv, ("snode", "rhs"), [(16 * a + b, 16 * b + a) for a in range(16) for b in range(16)])
    right = exchange_z(jnp.broadcast_to(top_inv[None], (8, *top_inv.shape)))
    a1, b1 = around(first, along_y), around(second, along_x)
    near_a = jnp.concatenate([first, *a1, *far(*a1, along_y)], axis=0)
    near_b = jnp.concatenate([second, *b1, *far(*b1, along_x)], axis=0)
    near_a, near_b, across, right = lax.optimization_barrier((near_a, near_b, across, right))
    a2, b2 = around(near_a, along_x), around(near_b, along_y)
    pieces = [near_a, *a2, *far(*a2, along_x), near_b, *b2, *far(*b2, along_y)]
    return pieces, across, right.reshape(2048, 256)


def exchange_z(a):
    return lax.all_to_all(a, "snode", 0, 0, axis_index_groups=Z_GROUPS)


def onward(a, d):
    return lax.ppermute(a, "snode", [(i, (i + 2 * d) % 16 if i % 2 == 0 else (i - 2 * d) % 16) for i in range(16)])


def sum_slot(chip, own_core, z, c):
    ahead = jnp.where(c == 0, chip - z, z - chip) % 8
    keep = jnp.where(ahead % 4 == 0, own_core, ahead < 4)
    distance = jnp.where(ahead < 4, ahead, 8 - ahead)
    second = jnp.where(keep == own_core, 0, 256)
    slot = jnp.where(distance == 0, 0, jnp.where(distance == 4, 1792, distance * 512 - 256 + second))
    return jnp.where(keep, slot, 2048 + slot)


def sum_z(keep, give):
    chip = keep.astype(F32) + swap_core(give).astype(F32)
    third, fourth, first = onward(chip[1280:1792].astype(BF), 1), onward(chip[1792:].astype(BF), 2), onward(chip[256:768].astype(BF), 1)
    second = chip[768:1280] + third.astype(F32)
    second = jnp.concatenate([second[:256] + fourth.astype(F32), second[256:]], axis=0).astype(BF)
    side = first.astype(F32) + onward(second, 2).astype(F32)
    return chip[:256] + side[:256] + swap_core(side[256:])


def gather_z(a):
    rows = a.shape[0]
    chip = jnp.concatenate([a, swap_core(a)], axis=0)
    second = onward(chip, 2)
    first = onward(chip, 1)
    third = onward(second, 1)
    fourth = onward(second[:rows], 2)
    side = jnp.concatenate([first, second, third, fourth], axis=0)
    return chip, side, swap_core(side)


def gathered_blocks(z, c):
    up = 1 - 2 * c
    yield 0, 0, z, c
    yield 0, 256, z, 1 - c
    for d in (1, 2, 3):
        below, above = lax.rem(z - d * up + 8, 8), lax.rem(z + d * up + 8, 8)
        yield 1, (d - 1) * 512, below, c
        yield 1, (d - 1) * 512 + 256, below, 1 - c
        yield 2, (d - 1) * 512, above, 1 - c
        yield 2, (d - 1) * 512 + 256, above, c
    yield 1, 1536, lax.rem(z + 4, 8), c
    yield 2, 1536, lax.rem(z + 4, 8), 1 - c


def gathered_slot(chip, own_core, z, c):
    ahead = jnp.where(c == 0, chip - z, z - chip) % 8
    own, away = jnp.where(own_core, 0, 256), jnp.where(own_core, 256, 0)
    middle = jnp.where(own_core, 512 + 1536, 2304 + 1536)
    slot = jnp.where(ahead < 4, 2304 + (ahead - 1) * 512 + away, 512 + (7 - ahead) * 512 + own)
    return jnp.where(ahead == 0, own, jnp.where(ahead == 4, middle, slot))


def each_block(pieces, x, y, per):
    for half in range(2):
        group = pieces[5 * half : 5 * half + 5]
        for far in range(4):
            for near in range(4):
                if far < 3:
                    piece, at = group[far], near * per
                else:
                    piece, at = (group[3], near * per) if near < 2 else (group[4], (near - 2) * per)
                a, b = (OFFSETS[far], OFFSETS[near]) if half == 0 else (OFFSETS[near], OFFSETS[far])
                yield half, piece, at, lax.rem(x + a, 4), lax.rem(y + b, 4)


def place_rows(rows, values, out, base):
    @pl.loop(0, 2)
    def _(block):
        total = None
        for k in range(8):
            target = rows[0:1, k * 512 : k * 512 + 512] - (block * 1024 + base)
            hit = lax.broadcasted_iota(jnp.int32, (1024, 512), 0) == target
            term = jnp.dot(
                hit.astype(F32).astype(BF), values[k * 512 : k * 512 + 512, :], preferred_element_type=F32
            )
            total = term if total is None else total + term
        out[pl.ds(pl.multiple_of(block * 1024, 1024), 1024), :] = total.astype(BF)


def forward_kernel(place, rows, loads, *refs):
    pieces, (inv, panel, forward, keep, give, partial_value) = refs[:10], refs[10:]
    x, y = place[2], place[3]
    for half, piece, at, bx, by in each_block(pieces, x, y, 2):
        r = 4 * bx + by
        for leaf in range(2):
            inv[2 * half + leaf, pl.ds(pl.multiple_of(r * 32, 32), 32), :] = piece[at + leaf, :32, :]
            panel[2 * half + leaf, pl.ds(pl.multiple_of(r * 64, 64), 64), :] = piece[at + leaf, 32:, :]
    for leaf in range(4):
        value = jnp.dot(inv[leaf], loads[leaf], preferred_element_type=F32).astype(BF)
        forward[leaf] = value
        partial_value[leaf * 1024 : leaf * 1024 + 1024, :] = jnp.dot(
            panel[leaf], value, preferred_element_type=F32
        ).astype(BF)

    place_rows(rows, partial_value, give, 2048)
    place_rows(rows, partial_value, keep, 0)


def square_kernel(place, after, left, right, right_other, out, total):
    c = place[1]
    for chip in range(8):
        for core, part in ((c, right), (1 - c, right_other)):
            first = pl.multiple_of((2 * chip + core) * 256, 256)
            total[pl.ds(first, 256), :] = part[chip * 256 : chip * 256 + 256, :]
    out[...] = lax.dot_general(
        left[...], total[...], (((0,), (0,)), ((), ())), preferred_element_type=F32
    ).astype(BF)


def top_kernel(place, own_chip, side, side_other, square, out, rounded, row_block, reduced):
    z, c = place[0], place[1]
    for k in range(16):
        row_block[:, k * 256 : k * 256 + 256] = square[k * 256 : k * 256 + 256, :]
    pieces = (own_chip, side, side_other)
    for piece, at, chip, core in gathered_blocks(z, c):
        first = pl.multiple_of((2 * chip + core) * 256, 256)
        reduced[pl.ds(first, 256), :] = pieces[piece][at : at + 256, :]
    value = jnp.dot(row_block[...], reduced[...], preferred_element_type=F32)
    out[...] = value
    rounded[...] = value.astype(BF)


def backward_kernel(rows, inv, panel, forward, own_chip, side, side_other, out, top, picked):
    top[:512, :] = own_chip[...].astype(F32)
    top[512:2304, :] = side[...].astype(F32)
    top[2304:, :] = side_other[...].astype(F32)
    for leaf in range(4):

        @pl.loop(0, 1024 // 64)
        def _(step):
            for part in range(4):
                first = pl.multiple_of(step * 64 + part * 16, 16)
                found = [top[pl.ds(rows[leaf * 1024 + first + k], 1), :] for k in range(16)]
                picked[pl.ds(first, 16), :] = jnp.concatenate(found, axis=0).astype(BF)

        through = lax.dot_general(panel[leaf], picked[...], (((0,), (0,)), ((), ())), preferred_element_type=F32)
        value = (forward[leaf].astype(F32) - through).astype(BF)
        out[leaf] = lax.dot_general(inv[leaf], value, (((0,), (0,)), ((), ())), preferred_element_type=F32)


def per_device(leaf_inv, leaf_panel, leaf_rows, leaf_loads, top_inv, top_loads):
    s, r = lax.axis_index("snode"), lax.axis_index("rhs")
    z, c, x, y = s // 2, s % 2, r // 4, r % 4
    place = jnp.stack([z, c, x, y]).astype(jnp.int32)
    own_core = ((leaf_rows // 256) % 2) == c
    chips, within = leaf_rows // 512, leaf_rows % 256
    slots = (sum_slot(chips, own_core, z, c) + within).reshape(-1)
    picks = (gathered_slot(chips, own_core, z, c) + within).reshape(-1)

    factors = jnp.concatenate([leaf_inv, leaf_panel], axis=1)
    pieces, across, right = gather_factors(factors[:2], factors[2:], top_inv)
    left = lax.all_gather(across, "rhs", axis=0, tiled=True)
    right_other = swap_core(right)
    inv, panel, forward, keep, give = pl.pallas_call(
        forward_kernel,
        out_shape=(
            jax.ShapeDtypeStruct((4, 512, 512), BF),
            jax.ShapeDtypeStruct((4, 1024, 512), BF),
            jax.ShapeDtypeStruct((4, 512, 256), BF),
            jax.ShapeDtypeStruct((2048, 256), BF),
            jax.ShapeDtypeStruct((2048, 256), BF),
        ),
        in_specs=[SMEM] + [VMEM] * 12,
        out_specs=[VMEM] * 5,
        scratch_shapes=[pltpu.VMEM((4096, 256), BF)],
        compiler_params=grant(26),
        cost_estimate=pl.CostEstimate(flops=10**10, bytes_accessed=20 * 2**20, transcendentals=0),
        name="leaf_forward",
    )(place, jnp.broadcast_to(slots[None], (8, 4096)), leaf_loads, *pieces)

    square = pl.pallas_call(
        square_kernel,
        out_shape=jax.ShapeDtypeStruct((256, 256), BF),
        in_specs=[SMEM, ANY] + [VMEM] * 3,
        out_specs=VMEM,
        scratch_shapes=[pltpu.VMEM((4096, 256), BF)],
        compiler_params=grant(12),
        cost_estimate=pl.CostEstimate(flops=10**9, bytes_accessed=6 * 2**20, transcendentals=0),
        name="top_square",
    )(place, forward, left, right, right_other)
    square_rows = lax.all_gather(square, "rhs", axis=0, tiled=True)

    reduced = (top_loads.astype(F32) - sum_z(keep, give)).astype(BF)
    reduced_pieces = gather_z(reduced)
    top_solution, top_rounded = pl.pallas_call(
        top_kernel,
        out_shape=(jax.ShapeDtypeStruct((256, 256), F32), jax.ShapeDtypeStruct((256, 256), BF)),
        in_specs=[SMEM] + [VMEM] * 4,
        out_specs=[VMEM] * 2,
        scratch_shapes=[pltpu.VMEM((256, 4096), BF), pltpu.VMEM((4096, 256), BF)],
        compiler_params=grant(12),
        cost_estimate=pl.CostEstimate(flops=10**9, bytes_accessed=6 * 2**20, transcendentals=0),
        name="top_solve",
    )(place, *reduced_pieces, square_rows)
    top_pieces = gather_z(top_rounded)
    leaf_solution = pl.pallas_call(
        backward_kernel,
        out_shape=jax.ShapeDtypeStruct((4, 512, 256), F32),
        in_specs=[SMEM] + [VMEM] * 6,
        out_specs=VMEM,
        scratch_shapes=[pltpu.VMEM((4096, 256), F32), pltpu.VMEM((1024, 256), BF)],
        compiler_params=grant(20),
        cost_estimate=pl.CostEstimate(flops=10**10, bytes_accessed=12 * 2**20, transcendentals=0),
        name="leaf_backward",
    )(picks, inv, panel, forward, *top_pieces)
    return leaf_solution, top_solution


def solution(mesh):
    return jax.shard_map(
        per_device,
        mesh=mesh,
        in_specs=(
            P("snode", "rhs", None),
            P("snode", "rhs", None),
            P("snode", None),
            P("snode", None, "rhs"),
            P("snode", "rhs"),
            P("snode", "rhs"),
        ),
        out_specs=(P("snode", None, "rhs"), P("snode", "rhs")),
        check_vma=False,
    )
```

```python
import jax
import jax.numpy as jnp
from jax import lax
from jax.experimental import pallas as pl
from jax.experimental.pallas import tpu as pltpu
from jax.sharding import PartitionSpec as P

BF = jnp.bfloat16
F32 = jnp.float32
OFFSETS = (0, 3, 1, 2)
XS, YS = 4, 4
Z_GROUPS = [[2 * z + c for z in range(8)] for c in range(2)]
VMEM = pl.BlockSpec(memory_space=pltpu.VMEM)
ANY = pl.BlockSpec(memory_space=pl.ANY)
SMEM = pl.BlockSpec(memory_space=pltpu.SMEM)


def grant(mebibytes):
    return pltpu.CompilerParams(vmem_limit_bytes=mebibytes * 1024 * 1024)


def move_rhs(a, dx, dy):
    pairs = [(4 * x + y, 4 * ((x + dx) % 4) + (y + dy) % 4) for x in range(XS) for y in range(YS)]
    return lax.ppermute(a, "rhs", pairs)


def swap_core(a):
    return lax.ppermute(a, "snode", [(i, i ^ 1) for i in range(16)])


def around(a, move):
    return move(a, 1), move(a, -1)


def far(before, after, move):
    half = before.shape[0] // 2
    return move(before[:half], 1), move(after[half:], -1)


def along_x(a, d):
    return move_rhs(a, d, 0)


def along_y(a, d):
    return move_rhs(a, 0, d)


def gather_factors(first, second, top_inv):
    a1, b1 = around(first, along_y), around(second, along_x)
    near_a = jnp.concatenate([first, *a1, *far(*a1, along_y)], axis=0)
    near_b = jnp.concatenate([second, *b1, *far(*b1, along_x)], axis=0)
    near_a, near_b, block = lax.optimization_barrier((near_a, near_b, top_inv))
    across = lax.ppermute(block, ("snode", "rhs"), [(16 * a + b, 16 * b + a) for a in range(16) for b in range(16)])
    a2, b2 = around(near_a, along_x), around(near_b, along_y)
    across, block = lax.optimization_barrier((across, block))
    right = exchange_z(jnp.broadcast_to(block[None], (8, *block.shape)))
    a2, b2, across = lax.optimization_barrier((a2, b2, across))
    pieces = [near_a, *a2, *far(*a2, along_x), near_b, *b2, *far(*b2, along_y)]
    return pieces, across, right.reshape(2048, 256)


def exchange_z(a):
    return lax.all_to_all(a, "snode", 0, 0, axis_index_groups=Z_GROUPS)


def onward(a, d):
    return lax.ppermute(a, "snode", [(i, (i + 2 * d) % 16 if i % 2 == 0 else (i - 2 * d) % 16) for i in range(16)])


def sum_slot(chip, own_core, z, c):
    ahead = jnp.where(c == 0, chip - z, z - chip) % 8
    keep = jnp.where(ahead % 4 == 0, own_core, ahead < 4)
    distance = jnp.where(ahead < 4, ahead, 8 - ahead)
    second = jnp.where(keep == own_core, 0, 256)
    slot = jnp.where(distance == 0, 0, jnp.where(distance == 4, 1792, distance * 512 - 256 + second))
    return jnp.where(keep, slot, 2048 + slot)


def sum_z(keep, given):
    chip = keep.astype(F32) + given.astype(F32)
    third, fourth, first = onward(chip[1280:1792].astype(BF), 1), onward(chip[1792:].astype(BF), 2), onward(chip[256:768].astype(BF), 1)
    second = chip[768:1280] + third.astype(F32)
    second = jnp.concatenate([second[:256] + fourth.astype(F32), second[256:]], axis=0).astype(BF)
    side = first.astype(F32) + onward(second, 2).astype(F32)
    return chip[:256] + side[:256] + swap_core(side[256:])


def gather_z(a):
    rows = a.shape[0]
    chip = jnp.concatenate([a, swap_core(a)], axis=0)
    second = onward(chip, 2)
    first = onward(chip, 1)
    third = onward(second, 1)
    fourth = onward(second[:rows], 2)
    side = jnp.concatenate([first, second, third, fourth], axis=0)
    return chip, side, swap_core(side)


def gathered_blocks(z, c):
    up = 1 - 2 * c
    yield 0, 0, z, c
    yield 0, 256, z, 1 - c
    for d in (1, 2, 3):
        below, above = lax.rem(z - d * up + 8, 8), lax.rem(z + d * up + 8, 8)
        yield 1, (d - 1) * 512, below, c
        yield 1, (d - 1) * 512 + 256, below, 1 - c
        yield 2, (d - 1) * 512, above, 1 - c
        yield 2, (d - 1) * 512 + 256, above, c
    yield 1, 1536, lax.rem(z + 4, 8), c
    yield 2, 1536, lax.rem(z + 4, 8), 1 - c


def gathered_slot(chip, own_core, z, c):
    ahead = jnp.where(c == 0, chip - z, z - chip) % 8
    own, away = jnp.where(own_core, 0, 256), jnp.where(own_core, 256, 0)
    middle = jnp.where(own_core, 512 + 1536, 2304 + 1536)
    slot = jnp.where(ahead < 4, 2304 + (ahead - 1) * 512 + away, 512 + (7 - ahead) * 512 + own)
    return jnp.where(ahead == 0, own, jnp.where(ahead == 4, middle, slot))


def each_block(pieces, x, y, per):
    for half in range(2):
        group = pieces[5 * half : 5 * half + 5]
        for far in range(4):
            for near in range(4):
                if far < 3:
                    piece, at = group[far], near * per
                else:
                    piece, at = (group[3], near * per) if near < 2 else (group[4], (near - 2) * per)
                a, b = (OFFSETS[far], OFFSETS[near]) if half == 0 else (OFFSETS[near], OFFSETS[far])
                yield half, piece, at, lax.rem(x + a, 4), lax.rem(y + b, 4)


def place_rows(rows, values, out, base):
    @pl.loop(0, 2)
    def _(block):
        total = None
        for k in range(8):
            target = rows[0:1, k * 512 : k * 512 + 512] - (block * 1024 + base)
            hit = lax.broadcasted_iota(jnp.int32, (1024, 512), 0) == target
            term = jnp.dot(
                hit.astype(F32).astype(BF), values[k * 512 : k * 512 + 512, :], preferred_element_type=F32
            )
            total = term if total is None else total + term
        out[pl.ds(pl.multiple_of(block * 1024, 1024), 1024), :] = total.astype(BF)


def forward_kernel(place, rows, loads, *refs):
    pieces, (inv, panel, forward, partial_value, give) = refs[:10], refs[10:]
    x, y = place[2], place[3]
    for half, piece, at, bx, by in each_block(pieces, x, y, 2):
        r = 4 * bx + by
        for leaf in range(2):
            inv[2 * half + leaf, pl.ds(pl.multiple_of(r * 32, 32), 32), :] = piece[at + leaf, :32, :]
            panel[2 * half + leaf, pl.ds(pl.multiple_of(r * 64, 64), 64), :] = piece[at + leaf, 32:, :]
    for leaf in range(4):
        value = jnp.dot(inv[leaf], loads[leaf], preferred_element_type=F32).astype(BF)
        forward[leaf] = value
        partial_value[leaf * 1024 : leaf * 1024 + 1024, :] = jnp.dot(
            panel[leaf], value, preferred_element_type=F32
        ).astype(BF)

    place_rows(rows, partial_value, give, 2048)


def keep_kernel(rows, partial_value, keep):
    place_rows(rows, partial_value, keep, 0)


def square_kernel(place, after, left, right, right_other, out, total):
    c = place[1]
    for chip in range(8):
        for core, part in ((c, right), (1 - c, right_other)):
            first = pl.multiple_of((2 * chip + core) * 256, 256)
            total[pl.ds(first, 256), :] = part[chip * 256 : chip * 256 + 256, :]
    out[...] = lax.dot_general(
        left[...], total[...], (((0,), (0,)), ((), ())), preferred_element_type=F32
    ).astype(BF)


def top_kernel(place, own_chip, side, side_other, square, out, rounded, row_block, reduced):
    z, c = place[0], place[1]
    for k in range(16):
        row_block[:, k * 256 : k * 256 + 256] = square[k * 256 : k * 256 + 256, :]
    pieces = (own_chip, side, side_other)
    for piece, at, chip, core in gathered_blocks(z, c):
        first = pl.multiple_of((2 * chip + core) * 256, 256)
        reduced[pl.ds(first, 256), :] = pieces[piece][at : at + 256, :]
    value = jnp.dot(row_block[...], reduced[...], preferred_element_type=F32)
    out[...] = value
    rounded[...] = value.astype(BF)


def backward_kernel(rows, inv, panel, forward, own_chip, side, side_other, out, top, picked):
    top[:512, :] = own_chip[...].astype(F32)
    top[512:2304, :] = side[...].astype(F32)
    top[2304:, :] = side_other[...].astype(F32)
    for leaf in range(4):

        @pl.loop(0, 1024 // 64)
        def _(step):
            for part in range(4):
                first = pl.multiple_of(step * 64 + part * 16, 16)
                found = [top[pl.ds(rows[leaf * 1024 + first + k], 1), :] for k in range(16)]
                picked[pl.ds(first, 16), :] = jnp.concatenate(found, axis=0).astype(BF)

        through = lax.dot_general(panel[leaf], picked[...], (((0,), (0,)), ((), ())), preferred_element_type=F32)
        value = (forward[leaf].astype(F32) - through).astype(BF)
        out[leaf] = lax.dot_general(inv[leaf], value, (((0,), (0,)), ((), ())), preferred_element_type=F32)


def per_device(leaf_inv, leaf_panel, leaf_rows, leaf_loads, top_inv, top_loads):
    s, r = lax.axis_index("snode"), lax.axis_index("rhs")
    z, c, x, y = s // 2, s % 2, r // 4, r % 4
    place = jnp.stack([z, c, x, y]).astype(jnp.int32)
    own_core = ((leaf_rows // 256) % 2) == c
    chips, within = leaf_rows // 512, leaf_rows % 256
    slots = (sum_slot(chips, own_core, z, c) + within).reshape(-1)
    picks = (gathered_slot(chips, own_core, z, c) + within).reshape(-1)

    factors = jnp.concatenate([leaf_inv, leaf_panel], axis=1)
    pieces, across, right = gather_factors(factors[:2], factors[2:], top_inv)
    left = lax.all_gather(across, "rhs", axis=0, tiled=True)
    rows = jnp.broadcast_to(slots[None], (8, 4096))
    inv, panel, forward, partial_value, give = pl.pallas_call(
        forward_kernel,
        out_shape=(
            jax.ShapeDtypeStruct((4, 512, 512), BF),
            jax.ShapeDtypeStruct((4, 1024, 512), BF),
            jax.ShapeDtypeStruct((4, 512, 256), BF),
            jax.ShapeDtypeStruct((4096, 256), BF),
            jax.ShapeDtypeStruct((2048, 256), BF),
        ),
        in_specs=[SMEM] + [VMEM] * 12,
        out_specs=[VMEM] * 5,
        compiler_params=grant(26),
        cost_estimate=pl.CostEstimate(flops=10**10, bytes_accessed=20 * 2**20, transcendentals=0),
        name="leaf_forward",
    )(place, rows, leaf_loads, *pieces)
    given = swap_core(give)
    keep = pl.pallas_call(
        keep_kernel,
        out_shape=jax.ShapeDtypeStruct((2048, 256), BF),
        in_specs=[VMEM] * 2,
        out_specs=VMEM,
        compiler_params=grant(12),
        cost_estimate=pl.CostEstimate(flops=5 * 10**9, bytes_accessed=3 * 2**20, transcendentals=0),
        name="leaf_keep",
    )(rows, partial_value)
    keep, given, right = lax.optimization_barrier((keep, given, right))
    right_other = swap_core(right)

    square = pl.pallas_call(
        square_kernel,
        out_shape=jax.ShapeDtypeStruct((256, 256), BF),
        in_specs=[SMEM, ANY] + [VMEM] * 3,
        out_specs=VMEM,
        scratch_shapes=[pltpu.VMEM((4096, 256), BF)],
        compiler_params=grant(12),
        cost_estimate=pl.CostEstimate(flops=10**9, bytes_accessed=6 * 2**20, transcendentals=0),
        name="top_square",
    )(place, forward, left, right, right_other)
    square_rows = lax.all_gather(square, "rhs", axis=0, tiled=True)

    reduced = (top_loads.astype(F32) - sum_z(keep, given)).astype(BF)
    reduced_pieces = gather_z(reduced)
    top_solution, top_rounded = pl.pallas_call(
        top_kernel,
        out_shape=(jax.ShapeDtypeStruct((256, 256), F32), jax.ShapeDtypeStruct((256, 256), BF)),
        in_specs=[SMEM] + [VMEM] * 4,
        out_specs=[VMEM] * 2,
        scratch_shapes=[pltpu.VMEM((256, 4096), BF), pltpu.VMEM((4096, 256), BF)],
        compiler_params=grant(12),
        cost_estimate=pl.CostEstimate(flops=10**9, bytes_accessed=6 * 2**20, transcendentals=0),
        name="top_solve",
    )(place, *reduced_pieces, square_rows)
    top_pieces = gather_z(top_rounded)
    leaf_solution = pl.pallas_call(
        backward_kernel,
        out_shape=jax.ShapeDtypeStruct((4, 512, 256), F32),
        in_specs=[SMEM] + [VMEM] * 6,
        out_specs=VMEM,
        scratch_shapes=[pltpu.VMEM((4096, 256), F32), pltpu.VMEM((1024, 256), BF)],
        compiler_params=grant(20),
        cost_estimate=pl.CostEstimate(flops=10**10, bytes_accessed=12 * 2**20, transcendentals=0),
        name="leaf_backward",
    )(picks, inv, panel, forward, *top_pieces)
    return leaf_solution, top_solution


def solution(mesh):
    return jax.shard_map(
        per_device,
        mesh=mesh,
        in_specs=(
            P("snode", "rhs", None),
            P("snode", "rhs", None),
            P("snode", None),
            P("snode", None, "rhs"),
            P("snode", "rhs"),
            P("snode", "rhs"),
        ),
        out_specs=(P("snode", None, "rhs"), P("snode", "rhs")),
        check_vma=False,
    )
```

```python
import jax
import jax.numpy as jnp
from jax import lax
from jax.experimental import pallas as pl
from jax.experimental.pallas import tpu as pltpu
from jax.sharding import PartitionSpec as P

BF = jnp.bfloat16
F32 = jnp.float32
OFFSETS = (0, 3, 1, 2)
XS, YS = 4, 4
Z_GROUPS = [[2 * z + c for z in range(8)] for c in range(2)]
VMEM = pl.BlockSpec(memory_space=pltpu.VMEM)
ANY = pl.BlockSpec(memory_space=pl.ANY)
SMEM = pl.BlockSpec(memory_space=pltpu.SMEM)


def grant(mebibytes):
    return pltpu.CompilerParams(vmem_limit_bytes=mebibytes * 1024 * 1024)


def move_rhs(a, dx, dy):
    pairs = [(4 * x + y, 4 * ((x + dx) % 4) + (y + dy) % 4) for x in range(XS) for y in range(YS)]
    return lax.ppermute(a, "rhs", pairs)


def swap_core(a):
    return lax.ppermute(a, "snode", [(i, i ^ 1) for i in range(16)])


def around(a, move):
    return move(a, 1), move(a, -1)


def far(before, after, move):
    half = before.shape[0] // 2
    return move(before[:half], 1), move(after[half:], -1)


def along_x(a, d):
    return move_rhs(a, d, 0)


def along_y(a, d):
    return move_rhs(a, 0, d)


def gather_factors(first, second, top_inv):
    across = lax.ppermute(top_inv, ("snode", "rhs"), [(16 * a + b, 16 * b + a) for a in range(16) for b in range(16)])
    a1, b1 = around(first, along_y), around(second, along_x)
    near_a = jnp.concatenate([first, *a1, *far(*a1, along_y)], axis=0)
    near_b = jnp.concatenate([second, *b1, *far(*b1, along_x)], axis=0)
    near_a, near_b, across = lax.optimization_barrier((near_a, near_b, across))
    a2, b2 = around(near_a, along_x), around(near_b, along_y)
    a2, b2, block = lax.optimization_barrier((a2, b2, top_inv))
    right = exchange_z(jnp.broadcast_to(block[None], (8, *block.shape)))
    pieces = [near_a, *a2, *far(*a2, along_x), near_b, *b2, *far(*b2, along_y)]
    return pieces, across, right.reshape(2048, 256)


def exchange_z(a):
    return lax.all_to_all(a, "snode", 0, 0, axis_index_groups=Z_GROUPS)


def onward(a, d):
    return lax.ppermute(a, "snode", [(i, (i + 2 * d) % 16 if i % 2 == 0 else (i - 2 * d) % 16) for i in range(16)])


def sum_slot(chip, own_core, z, c):
    ahead = jnp.where(c == 0, chip - z, z - chip) % 8
    keep = jnp.where(ahead % 4 == 0, own_core, ahead < 4)
    distance = jnp.where(ahead < 4, ahead, 8 - ahead)
    second = jnp.where(keep == own_core, 0, 256)
    slot = jnp.where(distance == 0, 0, jnp.where(distance == 4, 1792, distance * 512 - 256 + second))
    return jnp.where(keep, slot, 2048 + slot)


def sum_z(keep, given):
    def chip(first, last):
        return keep[first:last].astype(F32) + given[first:last].astype(F32)

    third, fourth = onward(chip(1280, 1792).astype(BF), 1), onward(chip(1792, 2048).astype(BF), 2)
    first = onward(chip(256, 768).astype(BF), 1)
    second = chip(768, 1280) + third.astype(F32)
    second = jnp.concatenate([second[:256] + fourth.astype(F32), second[256:]], axis=0).astype(BF)
    side = first.astype(F32) + onward(second, 2).astype(F32)
    return chip(0, 256) + side[:256] + swap_core(side[256:])


def gather_z(a):
    rows = a.shape[0]
    chip = jnp.concatenate([a, swap_core(a)], axis=0)
    second = onward(chip, 2)
    first = onward(chip, 1)
    third = onward(second, 1)
    fourth = onward(second[:rows], 2)
    side = jnp.concatenate([first, second, third, fourth], axis=0)
    return chip, side, swap_core(side)


def gathered_blocks(z, c):
    up = 1 - 2 * c
    yield 0, 0, z, c
    yield 0, 256, z, 1 - c
    for d in (1, 2, 3):
        below, above = lax.rem(z - d * up + 8, 8), lax.rem(z + d * up + 8, 8)
        yield 1, (d - 1) * 512, below, c
        yield 1, (d - 1) * 512 + 256, below, 1 - c
        yield 2, (d - 1) * 512, above, 1 - c
        yield 2, (d - 1) * 512 + 256, above, c
    yield 1, 1536, lax.rem(z + 4, 8), c
    yield 2, 1536, lax.rem(z + 4, 8), 1 - c


def gathered_slot(chip, own_core, z, c):
    ahead = jnp.where(c == 0, chip - z, z - chip) % 8
    own, away = jnp.where(own_core, 0, 256), jnp.where(own_core, 256, 0)
    middle = jnp.where(own_core, 512 + 1536, 2304 + 1536)
    slot = jnp.where(ahead < 4, 2304 + (ahead - 1) * 512 + away, 512 + (7 - ahead) * 512 + own)
    return jnp.where(ahead == 0, own, jnp.where(ahead == 4, middle, slot))


def each_block(pieces, x, y, per):
    for half in range(2):
        group = pieces[5 * half : 5 * half + 5]
        for far in range(4):
            for near in range(4):
                if far < 3:
                    piece, at = group[far], near * per
                else:
                    piece, at = (group[3], near * per) if near < 2 else (group[4], (near - 2) * per)
                a, b = (OFFSETS[far], OFFSETS[near]) if half == 0 else (OFFSETS[near], OFFSETS[far])
                yield half, piece, at, lax.rem(x + a, 4), lax.rem(y + b, 4)


def place_rows(rows, values, out, base):
    @pl.loop(0, 2)
    def _(block):
        total = None
        for k in range(8):
            target = rows[0:1, k * 512 : k * 512 + 512] - (block * 1024 + base)
            hit = lax.broadcasted_iota(jnp.int32, (1024, 512), 0) == target
            term = jnp.dot(
                hit.astype(F32).astype(BF), values[k * 512 : k * 512 + 512, :], preferred_element_type=F32
            )
            total = term if total is None else total + term
        out[pl.ds(pl.multiple_of(block * 1024, 1024), 1024), :] = total.astype(BF)


def forward_kernel(place, rows, loads, *refs):
    pieces, (inv, panel, forward, partial_value, give) = refs[:10], refs[10:]
    x, y = place[2], place[3]
    for half, piece, at, bx, by in each_block(pieces, x, y, 2):
        r = 4 * bx + by
        for leaf in range(2):
            inv[2 * half + leaf, pl.ds(pl.multiple_of(r * 32, 32), 32), :] = piece[at + leaf, :32, :]
            panel[2 * half + leaf, pl.ds(pl.multiple_of(r * 64, 64), 64), :] = piece[at + leaf, 32:, :]
    for leaf in range(4):
        value = jnp.dot(inv[leaf], loads[leaf], preferred_element_type=F32).astype(BF)
        forward[leaf] = value
        partial_value[leaf * 1024 : leaf * 1024 + 1024, :] = jnp.dot(
            panel[leaf], value, preferred_element_type=F32
        ).astype(BF)

    place_rows(rows, partial_value, give, 2048)


def keep_kernel(rows, partial_value, keep):
    place_rows(rows, partial_value, keep, 0)


def square_kernel(place, after, left, right, right_other, out, total):
    c = place[1]
    for chip in range(8):
        for core, part in ((c, right), (1 - c, right_other)):
            first = pl.multiple_of((2 * chip + core) * 256, 256)
            total[pl.ds(first, 256), :] = part[chip * 256 : chip * 256 + 256, :]
    out[...] = lax.dot_general(
        left[...], total[...], (((0,), (0,)), ((), ())), preferred_element_type=F32
    ).astype(BF)


def top_kernel(place, own_chip, side, side_other, square, out, rounded, row_block, reduced):
    z, c = place[0], place[1]
    for k in range(16):
        row_block[:, k * 256 : k * 256 + 256] = square[k * 256 : k * 256 + 256, :]
    pieces = (own_chip, side, side_other)
    for piece, at, chip, core in gathered_blocks(z, c):
        first = pl.multiple_of((2 * chip + core) * 256, 256)
        reduced[pl.ds(first, 256), :] = pieces[piece][at : at + 256, :]
    value = jnp.dot(row_block[...], reduced[...], preferred_element_type=F32)
    out[...] = value
    rounded[...] = value.astype(BF)


def backward_kernel(rows, inv, panel, forward, own_chip, side, side_other, out, top, picked):
    top[:512, :] = own_chip[...].astype(F32)
    top[512:2304, :] = side[...].astype(F32)
    top[2304:, :] = side_other[...].astype(F32)
    for leaf in range(4):

        @pl.loop(0, 1024 // 64)
        def _(step):
            for part in range(4):
                first = pl.multiple_of(step * 64 + part * 16, 16)
                found = [top[pl.ds(rows[leaf * 1024 + first + k], 1), :] for k in range(16)]
                picked[pl.ds(first, 16), :] = jnp.concatenate(found, axis=0).astype(BF)

        through = lax.dot_general(panel[leaf], picked[...], (((0,), (0,)), ((), ())), preferred_element_type=F32)
        value = (forward[leaf].astype(F32) - through).astype(BF)
        out[leaf] = lax.dot_general(inv[leaf], value, (((0,), (0,)), ((), ())), preferred_element_type=F32)


def per_device(leaf_inv, leaf_panel, leaf_rows, leaf_loads, top_inv, top_loads):
    s, r = lax.axis_index("snode"), lax.axis_index("rhs")
    z, c, x, y = s // 2, s % 2, r // 4, r % 4
    place = jnp.stack([z, c, x, y]).astype(jnp.int32)
    own_core = ((leaf_rows // 256) % 2) == c
    chips, within = leaf_rows // 512, leaf_rows % 256
    slots = (sum_slot(chips, own_core, z, c) + within).reshape(-1)
    picks = (gathered_slot(chips, own_core, z, c) + within).reshape(-1)

    factors = jnp.concatenate([leaf_inv, leaf_panel], axis=1)
    pieces, across, right = gather_factors(factors[:2], factors[2:], top_inv)
    left = lax.all_gather(across, "rhs", axis=0, tiled=True)
    rows = jnp.broadcast_to(slots[None], (8, 4096))
    inv, panel, forward, partial_value, give = pl.pallas_call(
        forward_kernel,
        out_shape=(
            jax.ShapeDtypeStruct((4, 512, 512), BF),
            jax.ShapeDtypeStruct((4, 1024, 512), BF),
            jax.ShapeDtypeStruct((4, 512, 256), BF),
            jax.ShapeDtypeStruct((4096, 256), BF),
            jax.ShapeDtypeStruct((2048, 256), BF),
        ),
        in_specs=[SMEM] + [VMEM] * 12,
        out_specs=[VMEM] * 5,
        compiler_params=grant(50),
        cost_estimate=pl.CostEstimate(flops=10**10, bytes_accessed=20 * 2**20, transcendentals=0),
        name="leaf_forward",
    )(place, rows, leaf_loads, *pieces)
    given = swap_core(give)
    keep = pl.pallas_call(
        keep_kernel,
        out_shape=jax.ShapeDtypeStruct((2048, 256), BF),
        in_specs=[VMEM] * 2,
        out_specs=VMEM,
        compiler_params=grant(50),
        cost_estimate=pl.CostEstimate(flops=5 * 10**9, bytes_accessed=3 * 2**20, transcendentals=0),
        name="leaf_keep",
    )(rows, partial_value)
    keep, given, right = lax.optimization_barrier((keep, given, right))
    right_other = swap_core(right)

    square = pl.pallas_call(
        square_kernel,
        out_shape=jax.ShapeDtypeStruct((256, 256), BF),
        in_specs=[SMEM, ANY] + [VMEM] * 3,
        out_specs=VMEM,
        scratch_shapes=[pltpu.VMEM((4096, 256), BF)],
        compiler_params=grant(50),
        cost_estimate=pl.CostEstimate(flops=10**9, bytes_accessed=6 * 2**20, transcendentals=0),
        name="top_square",
    )(place, forward, left, right, right_other)
    square_rows = lax.all_gather(square, "rhs", axis=0, tiled=True)

    reduced = (top_loads.astype(F32) - sum_z(keep, given)).astype(BF)
    reduced_pieces = gather_z(reduced)
    top_solution, top_rounded = pl.pallas_call(
        top_kernel,
        out_shape=(jax.ShapeDtypeStruct((256, 256), F32), jax.ShapeDtypeStruct((256, 256), BF)),
        in_specs=[SMEM] + [VMEM] * 4,
        out_specs=[VMEM] * 2,
        scratch_shapes=[pltpu.VMEM((256, 4096), BF), pltpu.VMEM((4096, 256), BF)],
        compiler_params=grant(50),
        cost_estimate=pl.CostEstimate(flops=10**9, bytes_accessed=6 * 2**20, transcendentals=0),
        name="top_solve",
    )(place, *reduced_pieces, square_rows)
    top_pieces = gather_z(top_rounded)
    leaf_solution = pl.pallas_call(
        backward_kernel,
        out_shape=jax.ShapeDtypeStruct((4, 512, 256), F32),
        in_specs=[SMEM] + [VMEM] * 6,
        out_specs=VMEM,
        scratch_shapes=[pltpu.VMEM((4096, 256), F32), pltpu.VMEM((1024, 256), BF)],
        compiler_params=grant(20),
        cost_estimate=pl.CostEstimate(flops=10**10, bytes_accessed=12 * 2**20, transcendentals=0),
        name="leaf_backward",
    )(picks, inv, panel, forward, *top_pieces)
    return leaf_solution, top_solution


def solution(mesh):
    return jax.shard_map(
        per_device,
        mesh=mesh,
        in_specs=(
            P("snode", "rhs", None),
            P("snode", "rhs", None),
            P("snode", None),
            P("snode", None, "rhs"),
            P("snode", "rhs"),
            P("snode", "rhs"),
        ),
        out_specs=(P("snode", None, "rhs"), P("snode", "rhs")),
        check_vma=False,
    )
```

```python
import jax
import jax.numpy as jnp
from jax import lax
from jax.experimental import pallas as pl
from jax.experimental.pallas import tpu as pltpu
from jax.sharding import PartitionSpec as P

BF = jnp.bfloat16
F32 = jnp.float32
OFFSETS = (0, 3, 1, 2)
XS, YS = 4, 4
VMEM = pl.BlockSpec(memory_space=pltpu.VMEM)
ANY = pl.BlockSpec(memory_space=pl.ANY)
SMEM = pl.BlockSpec(memory_space=pltpu.SMEM)


def grant(mebibytes):
    return pltpu.CompilerParams(vmem_limit_bytes=mebibytes * 1024 * 1024)


def move_rhs(a, dx, dy):
    pairs = [(4 * x + y, 4 * ((x + dx) % 4) + (y + dy) % 4) for x in range(XS) for y in range(YS)]
    return lax.ppermute(a, "rhs", pairs)


def swap_core(a):
    return lax.ppermute(a, "snode", [(i, i ^ 1) for i in range(16)])


def around(a, move):
    return move(a, 1), move(a, -1)


def far(before, after, move):
    half = before.shape[0] // 2
    return move(before[:half], 1), move(after[half:], -1)


def along_x(a, d):
    return move_rhs(a, d, 0)


def along_y(a, d):
    return move_rhs(a, 0, d)


def gather_factors(first, second, top_inv):
    across = lax.ppermute(top_inv, ("snode", "rhs"), [(16 * a + b, 16 * b + a) for a in range(16) for b in range(16)])
    a1, b1 = around(first, along_y), around(second, along_x)
    near_a = jnp.concatenate([first, *a1, *far(*a1, along_y)], axis=0)
    near_b = jnp.concatenate([second, *b1, *far(*b1, along_x)], axis=0)
    near_a, near_b, across, block = lax.optimization_barrier((near_a, near_b, across, top_inv))
    a2, b2 = around(near_a, along_x), around(near_b, along_y)
    chip = jnp.concatenate([block, swap_core(block)], axis=0)
    a2, b2, chip = lax.optimization_barrier((a2, b2, chip))
    near_side = onward(chip, 2), onward(chip, 1)
    pieces = [near_a, *a2, *far(*a2, along_x), near_b, *b2, *far(*b2, along_y)]
    *pieces, second, first = lax.optimization_barrier((*pieces, *near_side))
    return pieces, across, (chip, first, second, onward(second, 1), onward(second[:256], 2))


def onward(a, d):
    return lax.ppermute(a, "snode", [(i, (i + 2 * d) % 16 if i % 2 == 0 else (i - 2 * d) % 16) for i in range(16)])


def sum_slot(chip, own_core, z, c):
    ahead = jnp.where(c == 0, chip - z, z - chip) % 8
    keep = jnp.where(ahead % 4 == 0, own_core, ahead < 4)
    distance = jnp.where(ahead < 4, ahead, 8 - ahead)
    second = jnp.where(keep == own_core, 0, 256)
    slot = jnp.where(distance == 0, 0, jnp.where(distance == 4, 1792, distance * 512 - 256 + second))
    return jnp.where(keep, slot, 2048 + slot)


def sum_z(keep, given):
    def chip(first, last):
        return keep[first:last].astype(F32) + given[first:last].astype(F32)

    third, fourth = onward(chip(1280, 1792).astype(BF), 1), onward(chip(1792, 2048).astype(BF), 2)
    first = onward(chip(256, 768).astype(BF), 1)
    second = chip(768, 1280) + third.astype(F32)
    second = jnp.concatenate([second[:256] + fourth.astype(F32), second[256:]], axis=0).astype(BF)
    side = first.astype(F32) + onward(second, 2).astype(F32)
    return chip(0, 256) + side[:256] + swap_core(side[256:])


def gather_z(a):
    rows = a.shape[0]
    chip = jnp.concatenate([a, swap_core(a)], axis=0)
    second = onward(chip, 2)
    first = onward(chip, 1)
    third = onward(second, 1)
    fourth = onward(second[:rows], 2)
    side = jnp.concatenate([first, second, third, fourth], axis=0)
    return chip, side, swap_core(side)


def gathered_blocks(z, c):
    up = 1 - 2 * c
    yield 0, 0, z, c
    yield 0, 256, z, 1 - c
    for d in (1, 2, 3):
        below, above = lax.rem(z - d * up + 8, 8), lax.rem(z + d * up + 8, 8)
        yield 1, (d - 1) * 512, below, c
        yield 1, (d - 1) * 512 + 256, below, 1 - c
        yield 2, (d - 1) * 512, above, 1 - c
        yield 2, (d - 1) * 512 + 256, above, c
    yield 1, 1536, lax.rem(z + 4, 8), c
    yield 2, 1536, lax.rem(z + 4, 8), 1 - c


def gathered_slot(chip, own_core, z, c):
    ahead = jnp.where(c == 0, chip - z, z - chip) % 8
    own, away = jnp.where(own_core, 0, 256), jnp.where(own_core, 256, 0)
    middle = jnp.where(own_core, 512 + 1536, 2304 + 1536)
    slot = jnp.where(ahead < 4, 2304 + (ahead - 1) * 512 + away, 512 + (7 - ahead) * 512 + own)
    return jnp.where(ahead == 0, own, jnp.where(ahead == 4, middle, slot))


def each_block(pieces, x, y, per):
    for half in range(2):
        group = pieces[5 * half : 5 * half + 5]
        for far in range(4):
            for near in range(4):
                if far < 3:
                    piece, at = group[far], near * per
                else:
                    piece, at = (group[3], near * per) if near < 2 else (group[4], (near - 2) * per)
                a, b = (OFFSETS[far], OFFSETS[near]) if half == 0 else (OFFSETS[near], OFFSETS[far])
                yield half, piece, at, lax.rem(x + a, 4), lax.rem(y + b, 4)


def place_rows(rows, values, out, base):
    @pl.loop(0, 2)
    def _(block):
        total = None
        for k in range(8):
            target = rows[0:1, k * 512 : k * 512 + 512] - (block * 1024 + base)
            hit = lax.broadcasted_iota(jnp.int32, (1024, 512), 0) == target
            term = jnp.dot(
                hit.astype(F32).astype(BF), values[k * 512 : k * 512 + 512, :], preferred_element_type=F32
            )
            total = term if total is None else total + term
        out[pl.ds(pl.multiple_of(block * 1024, 1024), 1024), :] = total.astype(BF)


def forward_kernel(place, rows, loads, *refs):
    pieces, (inv, panel, forward, partial_value, give) = refs[:10], refs[10:]
    x, y = place[2], place[3]
    for half, piece, at, bx, by in each_block(pieces, x, y, 2):
        r = 4 * bx + by
        for leaf in range(2):
            inv[2 * half + leaf, pl.ds(pl.multiple_of(r * 32, 32), 32), :] = piece[at + leaf, :32, :]
            panel[2 * half + leaf, pl.ds(pl.multiple_of(r * 64, 64), 64), :] = piece[at + leaf, 32:, :]
    for leaf in range(4):
        value = jnp.dot(inv[leaf], loads[leaf], preferred_element_type=F32).astype(BF)
        forward[leaf] = value
        partial_value[leaf * 1024 : leaf * 1024 + 1024, :] = jnp.dot(
            panel[leaf], value, preferred_element_type=F32
        ).astype(BF)

    place_rows(rows, partial_value, give, 2048)


def keep_kernel(rows, partial_value, keep):
    place_rows(rows, partial_value, keep, 0)


def gathered_rows(place, pieces, out):
    for piece, at, chip, core in gathered_blocks(place[0], place[1]):
        first = pl.multiple_of((2 * chip + core) * 256, 256)
        out[pl.ds(first, 256), :] = pieces[piece][at : at + 256, :]


def square_kernel(place, after, left, own_chip, side, side_other, out, total):
    gathered_rows(place, (own_chip, side, side_other), total)
    out[...] = lax.dot_general(
        left[...], total[...], (((0,), (0,)), ((), ())), preferred_element_type=F32
    ).astype(BF)


def top_kernel(place, own_chip, side, side_other, square, out, rounded, row_block, reduced):
    for k in range(16):
        row_block[:, k * 256 : k * 256 + 256] = square[k * 256 : k * 256 + 256, :]
    gathered_rows(place, (own_chip, side, side_other), reduced)
    value = jnp.dot(row_block[...], reduced[...], preferred_element_type=F32)
    out[...] = value
    rounded[...] = value.astype(BF)


def backward_kernel(rows, inv, panel, forward, own_chip, side, side_other, out, top, picked):
    top[:512, :] = own_chip[...].astype(F32)
    top[512:2304, :] = side[...].astype(F32)
    top[2304:, :] = side_other[...].astype(F32)
    for leaf in range(4):

        @pl.loop(0, 1024 // 64)
        def _(step):
            for part in range(4):
                first = pl.multiple_of(step * 64 + part * 16, 16)
                found = [top[pl.ds(rows[leaf * 1024 + first + k], 1), :] for k in range(16)]
                picked[pl.ds(first, 16), :] = jnp.concatenate(found, axis=0).astype(BF)

        through = lax.dot_general(panel[leaf], picked[...], (((0,), (0,)), ((), ())), preferred_element_type=F32)
        value = (forward[leaf].astype(F32) - through).astype(BF)
        out[leaf] = lax.dot_general(inv[leaf], value, (((0,), (0,)), ((), ())), preferred_element_type=F32)


def per_device(leaf_inv, leaf_panel, leaf_rows, leaf_loads, top_inv, top_loads):
    s, r = lax.axis_index("snode"), lax.axis_index("rhs")
    z, c, x, y = s // 2, s % 2, r // 4, r % 4
    place = jnp.stack([z, c, x, y]).astype(jnp.int32)
    own_core = ((leaf_rows // 256) % 2) == c
    chips, within = leaf_rows // 512, leaf_rows % 256
    slots = (sum_slot(chips, own_core, z, c) + within).reshape(-1)
    picks = (gathered_slot(chips, own_core, z, c) + within).reshape(-1)

    factors = jnp.concatenate([leaf_inv, leaf_panel], axis=1)
    pieces, across, right = gather_factors(factors[:2], factors[2:], top_inv)
    left = lax.all_gather(across, "rhs", axis=0, tiled=True)
    rows = jnp.broadcast_to(slots[None], (8, 4096))
    inv, panel, forward, partial_value, give = pl.pallas_call(
        forward_kernel,
        out_shape=(
            jax.ShapeDtypeStruct((4, 512, 512), BF),
            jax.ShapeDtypeStruct((4, 1024, 512), BF),
            jax.ShapeDtypeStruct((4, 512, 256), BF),
            jax.ShapeDtypeStruct((4096, 256), BF),
            jax.ShapeDtypeStruct((2048, 256), BF),
        ),
        in_specs=[SMEM] + [VMEM] * 12,
        out_specs=[VMEM] * 5,
        compiler_params=grant(50),
        cost_estimate=pl.CostEstimate(flops=10**10, bytes_accessed=20 * 2**20, transcendentals=0),
        name="leaf_forward",
    )(place, rows, leaf_loads, *pieces)
    give, *right = lax.optimization_barrier((give, *right))
    given = swap_core(give)
    side = jnp.concatenate(right[1:], axis=0)
    side_other = swap_core(side)
    keep = pl.pallas_call(
        keep_kernel,
        out_shape=jax.ShapeDtypeStruct((2048, 256), BF),
        in_specs=[VMEM] * 2,
        out_specs=VMEM,
        compiler_params=grant(50),
        cost_estimate=pl.CostEstimate(flops=5 * 10**9, bytes_accessed=3 * 2**20, transcendentals=0),
        name="leaf_keep",
    )(rows, partial_value)
    keep, given, side_other = lax.optimization_barrier((keep, given, side_other))

    square = pl.pallas_call(
        square_kernel,
        out_shape=jax.ShapeDtypeStruct((256, 256), BF),
        in_specs=[SMEM, ANY] + [VMEM] * 4,
        out_specs=VMEM,
        scratch_shapes=[pltpu.VMEM((4096, 256), BF)],
        compiler_params=grant(50),
        cost_estimate=pl.CostEstimate(flops=10**9, bytes_accessed=6 * 2**20, transcendentals=0),
        name="top_square",
    )(place, forward, left, right[0], side, side_other)
    square_rows = lax.all_gather(square, "rhs", axis=0, tiled=True)

    reduced = (top_loads.astype(F32) - sum_z(keep, given)).astype(BF)
    reduced_pieces = gather_z(reduced)
    top_solution, top_rounded = pl.pallas_call(
        top_kernel,
        out_shape=(jax.ShapeDtypeStruct((256, 256), F32), jax.ShapeDtypeStruct((256, 256), BF)),
        in_specs=[SMEM] + [VMEM] * 4,
        out_specs=[VMEM] * 2,
        scratch_shapes=[pltpu.VMEM((256, 4096), BF), pltpu.VMEM((4096, 256), BF)],
        compiler_params=grant(50),
        cost_estimate=pl.CostEstimate(flops=10**9, bytes_accessed=6 * 2**20, transcendentals=0),
        name="top_solve",
    )(place, *reduced_pieces, square_rows)
    top_pieces = gather_z(top_rounded)
    leaf_solution = pl.pallas_call(
        backward_kernel,
        out_shape=jax.ShapeDtypeStruct((4, 512, 256), F32),
        in_specs=[SMEM] + [VMEM] * 6,
        out_specs=VMEM,
        scratch_shapes=[pltpu.VMEM((4096, 256), F32), pltpu.VMEM((1024, 256), BF)],
        compiler_params=grant(20),
        cost_estimate=pl.CostEstimate(flops=10**10, bytes_accessed=12 * 2**20, transcendentals=0),
        name="leaf_backward",
    )(picks, inv, panel, forward, *top_pieces)
    return leaf_solution, top_solution


def solution(mesh):
    return jax.shard_map(
        per_device,
        mesh=mesh,
        in_specs=(
            P("snode", "rhs", None),
            P("snode", "rhs", None),
            P("snode", None),
            P("snode", None, "rhs"),
            P("snode", "rhs"),
            P("snode", "rhs"),
        ),
        out_specs=(P("snode", None, "rhs"), P("snode", "rhs")),
        check_vma=False,
    )
```

```python
import jax
import jax.numpy as jnp
from jax import lax
from jax.experimental import pallas as pl
from jax.experimental.pallas import tpu as pltpu
from jax.sharding import PartitionSpec as P

BF = jnp.bfloat16
F32 = jnp.float32
OFFSETS = (0, 3, 1, 2)
XS, YS = 4, 4
Z_GROUPS = [[2 * z + c for z in range(8)] for c in range(2)]
VMEM = pl.BlockSpec(memory_space=pltpu.VMEM)
ANY = pl.BlockSpec(memory_space=pl.ANY)
SMEM = pl.BlockSpec(memory_space=pltpu.SMEM)
PARAMS = pltpu.CompilerParams(vmem_limit_bytes=50 * 1024 * 1024)
SMALL = pltpu.CompilerParams(vmem_limit_bytes=20 * 1024 * 1024)


def move_rhs(a, dx, dy):
    pairs = [(4 * x + y, 4 * ((x + dx) % 4) + (y + dy) % 4) for x in range(XS) for y in range(YS)]
    return lax.ppermute(a, "rhs", pairs)


def swap_core(a):
    return lax.ppermute(a, "snode", [(i, i ^ 1) for i in range(16)])


def around(a, move):
    return move(a, 1), move(a, -1)


def far(before, after, move):
    half = before.shape[0] // 2
    return move(before[:half], 1), move(after[half:], -1)


def along_x(a, d):
    return move_rhs(a, d, 0)


def along_y(a, d):
    return move_rhs(a, 0, d)


def gather_factors(first, second, top_inv):
    across = lax.ppermute(top_inv, ("snode", "rhs"), [(16 * a + b, 16 * b + a) for a in range(16) for b in range(16)])
    a1, b1 = around(first, along_y), around(second, along_x)
    near_a = jnp.concatenate([first, *a1, *far(*a1, along_y)], axis=0)
    near_b = jnp.concatenate([second, *b1, *far(*b1, along_x)], axis=0)
    near_a, near_b, across, top_inv = lax.optimization_barrier((near_a, near_b, across, top_inv))
    a2, b2 = around(near_a, along_x), around(near_b, along_y)
    right = exchange_z(jnp.broadcast_to(top_inv[None], (8, *top_inv.shape)))
    pieces = [near_a, *a2, *far(*a2, along_x), near_b, *b2, *far(*b2, along_y)]
    *pieces, right = lax.optimization_barrier((*pieces, right))
    return pieces, across, right.reshape(2048, 256)


def exchange_z(a):
    return lax.all_to_all(a, "snode", 0, 0, axis_index_groups=Z_GROUPS)


def onward(a, d):
    return lax.ppermute(a, "snode", [(i, (i + 2 * d) % 16 if i % 2 == 0 else (i - 2 * d) % 16) for i in range(16)])


def sum_slot(chip, own_core, z, c):
    ahead = jnp.where(c == 0, chip - z, z - chip) % 8
    keep = jnp.where(ahead % 4 == 0, own_core, ahead < 4)
    distance = jnp.where(ahead < 4, ahead, 8 - ahead)
    second = jnp.where(keep == own_core, 0, 256)
    slot = jnp.where(distance == 0, 0, jnp.where(distance == 4, 1792, distance * 512 - 256 + second))
    return jnp.where(keep, slot, 2048 + slot)


def sum_z(keep, give):
    given = swap_core(give)

    def chip(first, last):
        return keep[first:last].astype(F32) + given[first:last].astype(F32)

    third, fourth = onward(chip(1280, 1792).astype(BF), 1), onward(chip(1792, 2048).astype(BF), 2)
    first = onward(chip(256, 768).astype(BF), 1)
    second = chip(768, 1280) + third.astype(F32)
    second = jnp.concatenate([second[:256] + fourth.astype(F32), second[256:]], axis=0).astype(BF)
    side = first.astype(F32) + onward(second, 2).astype(F32)
    return chip(0, 256) + side[:256] + swap_core(side[256:])


def gather_z(a):
    rows = a.shape[0]
    chip = jnp.concatenate([a, swap_core(a)], axis=0)
    second = onward(chip, 2)
    first = onward(chip, 1)
    third = onward(second, 1)
    fourth = onward(second[:rows], 2)
    side = jnp.concatenate([first, second, third, fourth], axis=0)
    return chip, side, swap_core(side)


def gathered_blocks(z, c):
    up = 1 - 2 * c
    yield 0, 0, z, c
    yield 0, 256, z, 1 - c
    for d in (1, 2, 3):
        below, above = lax.rem(z - d * up + 8, 8), lax.rem(z + d * up + 8, 8)
        yield 1, (d - 1) * 512, below, c
        yield 1, (d - 1) * 512 + 256, below, 1 - c
        yield 2, (d - 1) * 512, above, 1 - c
        yield 2, (d - 1) * 512 + 256, above, c
    yield 1, 1536, lax.rem(z + 4, 8), c
    yield 2, 1536, lax.rem(z + 4, 8), 1 - c


def gathered_slot(chip, own_core, z, c):
    ahead = jnp.where(c == 0, chip - z, z - chip) % 8
    own, away = jnp.where(own_core, 0, 256), jnp.where(own_core, 256, 0)
    middle = jnp.where(own_core, 512 + 1536, 2304 + 1536)
    slot = jnp.where(ahead < 4, 2304 + (ahead - 1) * 512 + away, 512 + (7 - ahead) * 512 + own)
    return jnp.where(ahead == 0, own, jnp.where(ahead == 4, middle, slot))


def each_block(pieces, x, y, per):
    for half in range(2):
        group = pieces[5 * half : 5 * half + 5]
        for far in range(4):
            for near in range(4):
                if far < 3:
                    piece, at = group[far], near * per
                else:
                    piece, at = (group[3], near * per) if near < 2 else (group[4], (near - 2) * per)
                a, b = (OFFSETS[far], OFFSETS[near]) if half == 0 else (OFFSETS[near], OFFSETS[far])
                yield half, piece, at, lax.rem(x + a, 4), lax.rem(y + b, 4)


def place_rows(rows, values, out, base):
    @pl.loop(0, 2)
    def _(block):
        total = None
        for k in range(8):
            target = rows[0:1, k * 512 : k * 512 + 512] - (block * 1024 + base)
            hit = lax.broadcasted_iota(jnp.int32, (1024, 512), 0) == target
            term = jnp.dot(
                hit.astype(F32).astype(BF), values[k * 512 : k * 512 + 512, :], preferred_element_type=F32
            )
            total = term if total is None else total + term
        out[pl.ds(pl.multiple_of(block * 1024, 1024), 1024), :] = total.astype(BF)


def forward_kernel(place, rows, loads, *refs):
    pieces, (inv, panel, forward, keep, give, partial_value) = refs[:10], refs[10:]
    x, y = place[2], place[3]
    for half, piece, at, bx, by in each_block(pieces, x, y, 2):
        r = 4 * bx + by
        for leaf in range(2):
            inv[2 * half + leaf, pl.ds(pl.multiple_of(r * 32, 32), 32), :] = piece[at + leaf, :32, :]
            panel[2 * half + leaf, pl.ds(pl.multiple_of(r * 64, 64), 64), :] = piece[at + leaf, 32:, :]
    for leaf in range(4):
        value = jnp.dot(inv[leaf], loads[leaf], preferred_element_type=F32).astype(BF)
        forward[leaf] = value
        partial_value[leaf * 1024 : leaf * 1024 + 1024, :] = jnp.dot(
            panel[leaf], value, preferred_element_type=F32
        ).astype(BF)

    place_rows(rows, partial_value, give, 2048)
    place_rows(rows, partial_value, keep, 0)


def square_kernel(place, after, left, right, right_other, out, total):
    c = place[1]
    for chip in range(8):
        for core, part in ((c, right), (1 - c, right_other)):
            first = pl.multiple_of((2 * chip + core) * 256, 256)
            total[pl.ds(first, 256), :] = part[chip * 256 : chip * 256 + 256, :]
    out[...] = lax.dot_general(
        left[...], total[...], (((0,), (0,)), ((), ())), preferred_element_type=F32
    ).astype(BF)


def top_kernel(place, own_chip, side, side_other, square, out, rounded, row_block, reduced):
    z, c = place[0], place[1]
    for k in range(16):
        row_block[:, k * 256 : k * 256 + 256] = square[k * 256 : k * 256 + 256, :]
    pieces = (own_chip, side, side_other)
    for piece, at, chip, core in gathered_blocks(z, c):
        first = pl.multiple_of((2 * chip + core) * 256, 256)
        reduced[pl.ds(first, 256), :] = pieces[piece][at : at + 256, :]
    value = jnp.dot(row_block[...], reduced[...], preferred_element_type=F32)
    out[...] = value
    rounded[...] = value.astype(BF)


def backward_kernel(rows, inv, panel, forward, own_chip, side, side_other, out, top, picked):
    top[:512, :] = own_chip[...].astype(F32)
    top[512:2304, :] = side[...].astype(F32)
    top[2304:, :] = side_other[...].astype(F32)
    for leaf in range(4):

        @pl.loop(0, 1024 // 64)
        def _(step):
            for part in range(4):
                first = pl.multiple_of(step * 64 + part * 16, 16)
                found = [top[pl.ds(rows[leaf * 1024 + first + k], 1), :] for k in range(16)]
                picked[pl.ds(first, 16), :] = jnp.concatenate(found, axis=0).astype(BF)

        through = lax.dot_general(panel[leaf], picked[...], (((0,), (0,)), ((), ())), preferred_element_type=F32)
        value = (forward[leaf].astype(F32) - through).astype(BF)
        out[leaf] = lax.dot_general(inv[leaf], value, (((0,), (0,)), ((), ())), preferred_element_type=F32)


def per_device(leaf_inv, leaf_panel, leaf_rows, leaf_loads, top_inv, top_loads):
    s, r = lax.axis_index("snode"), lax.axis_index("rhs")
    z, c, x, y = s // 2, s % 2, r // 4, r % 4
    place = jnp.stack([z, c, x, y]).astype(jnp.int32)
    own_core = ((leaf_rows // 256) % 2) == c
    chips, within = leaf_rows // 512, leaf_rows % 256
    slots = (sum_slot(chips, own_core, z, c) + within).reshape(-1)
    picks = (gathered_slot(chips, own_core, z, c) + within).reshape(-1)

    factors = jnp.concatenate([leaf_inv, leaf_panel], axis=1)
    pieces, across, right = gather_factors(factors[:2], factors[2:], top_inv)
    left = lax.all_gather(across, "rhs", axis=0, tiled=True)
    right_other = swap_core(right)
    inv, panel, forward, keep, give = pl.pallas_call(
        forward_kernel,
        out_shape=(
            jax.ShapeDtypeStruct((4, 512, 512), BF),
            jax.ShapeDtypeStruct((4, 1024, 512), BF),
            jax.ShapeDtypeStruct((4, 512, 256), BF),
            jax.ShapeDtypeStruct((2048, 256), BF),
            jax.ShapeDtypeStruct((2048, 256), BF),
        ),
        in_specs=[SMEM] + [VMEM] * 12,
        out_specs=[VMEM] * 5,
        scratch_shapes=[pltpu.VMEM((4096, 256), BF)],
        compiler_params=PARAMS,
        cost_estimate=pl.CostEstimate(flops=10**10, bytes_accessed=20 * 2**20, transcendentals=0),
        name="leaf_forward",
    )(place, jnp.broadcast_to(slots[None], (8, 4096)), leaf_loads, *pieces)

    square = pl.pallas_call(
        square_kernel,
        out_shape=jax.ShapeDtypeStruct((256, 256), BF),
        in_specs=[SMEM, ANY] + [VMEM] * 3,
        out_specs=VMEM,
        scratch_shapes=[pltpu.VMEM((4096, 256), BF)],
        compiler_params=PARAMS,
        cost_estimate=pl.CostEstimate(flops=10**9, bytes_accessed=6 * 2**20, transcendentals=0),
        name="top_square",
    )(place, forward, left, right, right_other)
    square_rows = lax.all_gather(square, "rhs", axis=0, tiled=True)

    reduced = (top_loads.astype(F32) - sum_z(keep, give)).astype(BF)
    reduced_pieces = gather_z(reduced)
    top_solution, top_rounded = pl.pallas_call(
        top_kernel,
        out_shape=(jax.ShapeDtypeStruct((256, 256), F32), jax.ShapeDtypeStruct((256, 256), BF)),
        in_specs=[SMEM] + [VMEM] * 4,
        out_specs=[VMEM] * 2,
        scratch_shapes=[pltpu.VMEM((256, 4096), BF), pltpu.VMEM((4096, 256), BF)],
        compiler_params=PARAMS,
        cost_estimate=pl.CostEstimate(flops=10**9, bytes_accessed=6 * 2**20, transcendentals=0),
        name="top_solve",
    )(place, *reduced_pieces, square_rows)
    top_pieces = gather_z(top_rounded)
    leaf_solution = pl.pallas_call(
        backward_kernel,
        out_shape=jax.ShapeDtypeStruct((4, 512, 256), F32),
        in_specs=[SMEM] + [VMEM] * 6,
        out_specs=VMEM,
        scratch_shapes=[pltpu.VMEM((4096, 256), F32), pltpu.VMEM((1024, 256), BF)],
        compiler_params=SMALL,
        cost_estimate=pl.CostEstimate(flops=10**10, bytes_accessed=12 * 2**20, transcendentals=0),
        name="leaf_backward",
    )(picks, inv, panel, forward, *top_pieces)
    return leaf_solution, top_solution


def solution(mesh):
    return jax.shard_map(
        per_device,
        mesh=mesh,
        in_specs=(
            P("snode", "rhs", None),
            P("snode", "rhs", None),
            P("snode", None),
            P("snode", None, "rhs"),
            P("snode", "rhs"),
            P("snode", "rhs"),
        ),
        out_specs=(P("snode", None, "rhs"), P("snode", "rhs")),
        check_vma=False,
    )
```
